256 devices in a mesh: lat: 4 (over y_lo, core), lon: 64 (over y_hi, x, z).
Axes of the slice: x: 4, y: 4 (y_hi: 2, y_lo: 2; y = y_hi * 2 + y_lo), z: 8, core: 2. Of those that a mesh axis runs over, the one named last changes fastest.
Arguments:
- latent: bfloat16 [64, 1024, 384], P('lat', 'lon'), may hold values from -6 to 6
- cotangent: bfloat16 [64, 1024, 384], P('lat', 'lon'), may hold values from -6 to 6
- gain_attn: float32 [384], replicated, may hold values from 0.1 to 1.9
- w_qkv: bfloat16 [384, 1152], replicated, may hold values from -0.3125 to 0.3125
- rel_bias: float32 [6, 7, 7], replicated, may hold values from -4 to 4
- w_out: bfloat16 [384, 384], replicated, may hold values from -0.3125 to 0.3125
- gain_mlp: float32 [384], replicated, may hold values from 0.1 to 1.9
- w_fc1: bfloat16 [384, 1536], replicated, may hold values from -0.3125 to 0.3125
- w_fc2: bfloat16 [1536, 384], replicated, may hold values from -0.15625 to 0.15625
Outputs:
- output: bfloat16 [64, 1024, 384], P('lat', 'lon')
- d_latent: bfloat16 [64, 1024, 384], P('lat', 'lon')
- d_qkv: float32 [384, 1152], replicated
- d_out: float32 [384, 384], replicated
- d_fc1: float32 [384, 1536], replicated
- d_fc2: float32 [1536, 384], replicated
- d_rel: float32 [6, 7, 7], replicated
- d_gain_attn: float32 [384], replicated
- d_gain_mlp: float32 [384], replicated
The draws below stay inside these ranges and needn't reach their ends.
All inputs are finite; a program needn't handle non-finite values.
Results may differ from the reference program's by a relative error of at most 0.022.
Values may be sent and summed in bfloat16 or wider, within the bound.
No kernel may reach another device: no remote copies, remote signals or barrier semaphores. Data moves between devices by JAX's collectives and lax.ppermute only.
A program may use at most 192 MiB of HBM per device.

```python
import jax
import jax.numpy as jnp
from jax import lax

D = 384
HEADS = 6
HEAD = 64
FF = 1536
CLAT = 16
CLON = 16
NLAT = 64
NLON = 1024


def steps_of(key, dims, split, smallest, largest):
    level = 1.0
    for dim, parts in split:
        heights = jax.random.uniform(jax.random.fold_in(jax.random.fold_in(key, 6), dim), (parts,), jnp.float32, smallest / len(split), largest / len(split))
        level = level * jnp.repeat(jnp.exp(heights), dims[dim] // parts).reshape((-1,) + (1,) * (len(dims) - 1 - dim))
    return level


def bell_draw(rng, shape, scale, bound, pieces=(), kind=jnp.bfloat16):
    level = steps_of(rng, shape, pieces, -0.22, 0.18) if pieces else 1.0
    array = jax.random.normal(rng, shape, jnp.float32) * scale * level
    return jnp.minimum(jnp.maximum(array, -bound), bound).astype(kind)


def setup_inputs(seed: int = 0) -> dict:
    key_list = jax.random.split(jax.random.key(seed), 10)
    return {
        "latent": bell_draw(key_list[0], (NLAT, NLON, D), 1.0, 6.0, ((0, 4), (1, 64))),
        "cotangent": bell_draw(key_list[1], (NLAT, NLON, D), 1.0, 6.0, ((0, 4), (1, 64))),
        "gain_attn": jnp.clip(1.0 + 0.18 * jax.random.normal(key_list[2], (D,), jnp.float32), 0.1, 1.9),
        "w_qkv": bell_draw(key_list[3], (D, 3 * D), D ** -0.5, 0.3125),
        "rel_bias": bell_draw(key_list[4], (HEADS, 7, 7), 1.0, 4.0, (), jnp.float32),
        "w_out": bell_draw(key_list[5], (D, D), D ** -0.5, 0.3125),
        "gain_mlp": jnp.clip(1.0 + 0.18 * jax.random.normal(key_list[6], (D,), jnp.float32), 0.1, 1.9),
        "w_fc1": bell_draw(key_list[7], (D, FF), D ** -0.5, 0.3125),
        "w_fc2": bell_draw(key_list[8], (FF, D), FF ** -0.5, 0.15625),
    }


def layer_norm(values, gain):
    centre = lax.optimization_barrier(jnp.mean(values, -1, keepdims=True))
    centred = values - centre
    variance = lax.optimization_barrier(jnp.mean(centred * centred, -1, keepdims=True))
    return centred * lax.rsqrt(variance + 1e-05) * gain

def activate(values):
    return jax.nn.gelu(values, approximate=True)

def outer_sum(first_op, second_op):
    return lax.dot_general(first_op, second_op, (((0,), (0,)), ((), ())), preferred_element_type=jnp.float32)

def times_transposed(first_op, weight):
    return lax.dot_general(first_op, weight, (((1,), (1,)), ((), ())), preferred_element_type=jnp.float32)

def shifted_grid(field, tap_index, sign):
    lat_shift = (tap_index // 7 - 3) * CLAT * sign
    lon_shift = (tap_index % 7 - 3) * CLON * sign
    moved = jnp.roll(field, -lat_shift, axis=0)
    return jnp.roll(moved, -lon_shift, axis=1)

def reference(latent, cotangent, gain_attn, w_qkv, rel_bias, w_out, gain_mlp, w_fc1, w_fc2):
    lat_cells, lon_cells, width = latent.shape
    flat = latent.reshape(-1, width).astype(jnp.float32)
    normed, back_attn = jax.vjp(layer_norm, flat, gain_attn)
    normed_b = normed.astype(jnp.bfloat16)
    projected = jnp.dot(normed_b, w_qkv, preferred_element_type=jnp.float32)
    queries = projected[:, :width].astype(jnp.bfloat16)
    key_vals = projected[:, width:].astype(jnp.bfloat16)
    grid_shape = (lat_cells, lon_cells, HEADS, HEAD)
    query_grid = queries.astype(jnp.float32).reshape(grid_shape)
    key_grid = key_vals[:, :width].astype(jnp.float32).reshape(grid_shape)
    value_grid = key_vals[:, width:].astype(jnp.float32).reshape(grid_shape)
    scale = HEAD ** (-0.5)
    taps = jnp.arange(49, dtype=jnp.int32)
    bias_table = rel_bias.reshape(HEADS, 49)
    lat_index = jnp.arange(lat_cells, dtype=jnp.int32)[:, None, None]

    def score_tap(carry, tap_index):
        keys_here = shifted_grid(key_grid, tap_index, 1)
        score = lax.optimization_barrier(jnp.sum(query_grid * keys_here, -1)) * scale + bias_table[:, tap_index]
        return (carry, score)
    _, scores = lax.scan(score_tap, jnp.float32(0.0), taps)

    def inside(tap_index):
        target = lat_index + (tap_index // 7 - 3) * CLAT
        return (target >= 0) & (target < lat_cells)
    valid = jax.vmap(inside)(taps)
    weights = jnp.where(valid, jnp.exp(scores), 0.0)
    prob = weights / lax.optimization_barrier(jnp.sum(weights, 0, keepdims=True))
    prob_b = prob.astype(jnp.bfloat16)

    def mix_tap(total, tap_index):
        values_here = shifted_grid(value_grid, tap_index, 1)
        return (total + prob_b[tap_index].astype(jnp.float32)[..., None] * values_here, None)
    mixed, _ = lax.scan(mix_tap, jnp.zeros(grid_shape, jnp.float32), taps)
    mixed_b = mixed.reshape(-1, width).astype(jnp.bfloat16)
    resid = flat + jnp.dot(mixed_b, w_out, preferred_element_type=jnp.float32)
    normed_two, back_mlp = jax.vjp(layer_norm, resid, gain_mlp)
    normed_two_b = normed_two.astype(jnp.bfloat16)
    hidden = jnp.dot(normed_two_b, w_fc1, preferred_element_type=jnp.float32)
    active, back_act = jax.vjp(activate, hidden)
    active_b = active.astype(jnp.bfloat16)
    output = (resid + jnp.dot(active_b, w_fc2, preferred_element_type=jnp.float32)).astype(jnp.bfloat16)
    grad_out = cotangent.reshape(-1, width)
    d_fc2 = outer_sum(active_b, grad_out)
    d_active = times_transposed(grad_out, w_fc2)
    d_hidden = back_act(d_active)[0].astype(jnp.bfloat16)
    d_fc1 = outer_sum(normed_two_b, d_hidden)
    d_normed_two = times_transposed(d_hidden, w_fc1)
    d_resid_norm, d_gain_mlp = back_mlp(d_normed_two)
    d_resid = grad_out.astype(jnp.float32) + d_resid_norm
    d_resid_b = d_resid.astype(jnp.bfloat16)
    d_out = outer_sum(mixed_b, d_resid_b)
    d_mixed_b = times_transposed(d_resid_b, w_out).astype(jnp.bfloat16)
    d_mixed_grid = d_mixed_b.astype(jnp.float32).reshape(grid_shape)

    def slope_tap(carry, tap_index):
        values_here = shifted_grid(value_grid, tap_index, 1)
        return (carry, lax.optimization_barrier(jnp.sum(d_mixed_grid * values_here, -1)))
    _, d_prob = lax.scan(slope_tap, jnp.float32(0.0), taps)
    d_score = prob * (d_prob - lax.optimization_barrier(jnp.sum(prob * d_prob, 0, keepdims=True)))
    d_rel = lax.optimization_barrier(jnp.sum(d_score, (1, 2))).T.reshape(HEADS, 7, 7)
    d_score_b = (d_score * scale).astype(jnp.bfloat16)

    def back_tap(carry, tap_index):
        d_query, d_key, d_value = carry
        weight_here = d_score_b[tap_index].astype(jnp.float32)[..., None]
        d_query = d_query + weight_here * shifted_grid(key_grid, tap_index, 1)
        key_term = lax.optimization_barrier((weight_here * query_grid).astype(jnp.bfloat16)).astype(jnp.float32)
        value_term = lax.optimization_barrier((prob_b[tap_index].astype(jnp.float32)[..., None] * d_mixed_grid).astype(jnp.bfloat16)).astype(jnp.float32)
        d_key = d_key + shifted_grid(key_term, tap_index, -1)
        d_value = d_value + shifted_grid(value_term, tap_index, -1)
        return ((d_query, d_key, d_value), None)
    zero_grid = jnp.zeros(grid_shape, jnp.float32)
    (d_query, d_key, d_value), _ = lax.scan(back_tap, (zero_grid, zero_grid, zero_grid), taps)
    d_proj = jnp.concatenate([d_query.reshape(-1, width), d_key.reshape(-1, width), d_value.reshape(-1, width)], -1).astype(jnp.bfloat16)
    d_qkv = outer_sum(normed_b, d_proj)
    d_normed = times_transposed(d_proj, w_qkv)
    d_flat_norm, d_gain_attn = back_attn(d_normed)
    d_latent = (d_resid + d_flat_norm).astype(jnp.bfloat16).reshape(latent.shape)
    return (output.reshape(latent.shape), d_latent, d_qkv, d_out, d_fc1, d_fc2, d_rel, d_gain_attn, d_gain_mlp)
```

```python
import jax
import jax.numpy as jnp
from jax import lax
from jax.experimental import pallas as pl
from jax.experimental.pallas import tpu as pltpu
from jax.sharding import Mesh, PartitionSpec as P

HEADS = 6
HEAD = 64
D = 384
FF = 1536
BANDS = 4
SECTORS = 64
CELLS = BANDS * SECTORS
SCALE = HEAD ** (-0.5)
ABSENT = -1e30
AXES = ("y_lo", "core", "y_hi", "x", "z")
PLANE = ("y_lo", "y_hi", "x")

LANES = 128
HALF = 7168
PIECE = HALF // 16
PART = PIECE // 8
QKV_FIRST = 6
FC1_AT, QKV_AT, REL_AT = 0, 4608, 6912
FC2_AT, OUT_AT, QKV_REST_AT, GAIN_AT = 0, 4608, 5760, 6912

f32, bf16 = jnp.float32, jnp.bfloat16


def dot(a, b):
    return lax.dot_general(a, b, (((1,), (0,)), ((), ())), preferred_element_type=f32)


def dot_nt(a, b):
    return lax.dot_general(a, b, (((1,), (1,)), ((), ())), preferred_element_type=f32)


def dot_tn(a, b):
    return lax.dot_general(a, b, (((0,), (0,)), ((), ())), preferred_element_type=f32)


def norm(values):
    centred = values - jnp.mean(values, -1, keepdims=True)
    inverse = lax.rsqrt(jnp.mean(centred * centred, -1, keepdims=True) + 1e-05)
    return centred * inverse, inverse


def norm_back(d_normed, gain, unit, inverse):
    d_unit = d_normed * gain
    d_values = inverse * (
        d_unit
        - jnp.mean(d_unit, -1, keepdims=True)
        - unit * jnp.mean(d_unit * unit, -1, keepdims=True)
    )
    return d_values, jnp.sum(d_normed * unit, 0, keepdims=True)


def gelu_and_slope(x):
    root = 0.7978845608028654
    square = x * x
    t = jnp.tanh(root * x * (1.0 + 0.044715 * square))
    half = 0.5 * (1.0 + t)
    slope = half + (0.5 * root) * x * (1.0 - t * t) * (1.0 + 3.0 * 0.044715 * square)
    return x * half, slope


def store_columns(ref, half, at, values):
    rows, width = values.shape
    for block in range(width // LANES):
        ref[half, pl.ds(at + block * rows, rows), :] = values[:, block * LANES : (block + 1) * LANES].astype(bf16)


def block_kernel(x_ref, cot_ref, gain_attn_ref, w_qkv_ref, bias_ref, w_out_ref, gain_mlp_ref, w_fc1_ref, w_fc2_ref,
                 out_ref, d_latent_ref, grads_ref):
    x = x_ref[...].astype(f32)
    gain_attn = gain_attn_ref[...]
    unit, inverse = norm(x)
    normed = (unit * gain_attn).astype(bf16)
    projected = dot(normed, w_qkv_ref[...]).astype(bf16)

    lane = lax.broadcasted_iota(jnp.int32, (1, LANES), 1)
    low = lane < HEAD
    apart = (
        lax.broadcasted_iota(jnp.int32, (SECTORS, LANES), 1)
        - lax.broadcasted_iota(jnp.int32, (SECTORS, LANES), 0)
    ) & (SECTORS - 1)

    def one_head(pair, second):
        return jnp.where(low, jnp.bfloat16(0), pair) if second else jnp.where(low, pair, jnp.bfloat16(0))

    def pair_of(array, part, pair):
        start = part * D + pair * LANES
        return array[:, start : start + LANES]

    probs, probs_b, mixed = [], [], []
    for pair in range(HEADS // 2):
        query, key, value = (pair_of(projected, part, pair) for part in range(3))
        total = None
        for second in range(2):
            head = 2 * pair + second
            tiles = []
            for first in range(6):
                tile = jnp.full((SECTORS, LANES), ABSENT, f32)
                for step in range(7):
                    row = bias_ref[(head * 6 + first) * 7 + step : (head * 6 + first) * 7 + step + 1, :]
                    tile = jnp.where(apart == (step - 3) % SECTORS, row, tile)
                tiles.append(tile)
            bias = jnp.concatenate(
                [jnp.concatenate([tiles[2 * side - band + 3] for band in range(BANDS)], 0) for side in range(2)], 1
            )
            score = dot_nt(one_head(query, second), key) * SCALE + bias
            weight = jnp.exp(score)
            prob = weight / jnp.sum(weight, -1, keepdims=True)
            prob_b = prob.astype(bf16)
            probs.append(prob)
            probs_b.append(prob_b)
            part = dot(prob_b, one_head(value, second))
            total = part if total is None else total + part
        mixed.append(total.astype(bf16))
    mixed = jnp.concatenate(mixed, 1)

    resid = x + dot(mixed, w_out_ref[...])
    gain_mlp = gain_mlp_ref[...]
    unit_two, inverse_two = norm(resid)
    normed_two = (unit_two * gain_mlp).astype(bf16)
    hidden = dot(normed_two, w_fc1_ref[...])
    active, slope = gelu_and_slope(hidden)
    active = active.astype(bf16)
    out_ref[...] = (resid + dot(active, w_fc2_ref[...])).astype(bf16)

    cot = cot_ref[...]
    store_columns(grads_ref, 1, FC2_AT, dot_tn(active, cot))
    d_hidden = (dot_nt(cot, w_fc2_ref[...]) * slope).astype(bf16)
    store_columns(grads_ref, 0, FC1_AT, dot_tn(normed_two, d_hidden))
    d_normed_two = dot_nt(d_hidden, w_fc1_ref[...])
    d_values, d_gain_mlp = norm_back(d_normed_two, gain_mlp, unit_two, inverse_two)
    d_resid = cot.astype(f32) + d_values
    d_resid_b = d_resid.astype(bf16)
    store_columns(grads_ref, 1, OUT_AT, dot_tn(mixed, d_resid_b))
    d_mixed = dot_nt(d_resid_b, w_out_ref[...]).astype(bf16)

    d_queries, d_keys, d_values_ = [], [], []
    rel_rows = []
    for pair in range(HEADS // 2):
        query, key, value = (pair_of(projected, part, pair) for part in range(3))
        d_mixed_pair = pair_of(d_mixed, 0, pair)
        d_query = d_key = d_value = None
        for second in range(2):
            head = 2 * pair + second
            prob, prob_b = probs[head], probs_b[head]
            d_mixed_here = one_head(d_mixed_pair, second)
            d_prob = dot_nt(d_mixed_here, value)
            d_score = prob * (d_prob - jnp.sum(prob * d_prob, -1, keepdims=True))
            for first in range(6):
                tile = None
                for band in range(BANDS):
                    for side in range(2):
                        if 2 * side - band + 3 == first:
                            here = d_score[band * SECTORS : (band + 1) * SECTORS, side * LANES : (side + 1) * LANES]
                            tile = here if tile is None else tile + here
                for step in range(7):
                    rel_rows.append(jnp.sum(jnp.where(apart == (step - 3) % SECTORS, tile, 0.0), 0, keepdims=True))
            d_score_b = (d_score * SCALE).astype(bf16)
            parts = (
                dot(d_score_b, one_head(key, second)),
                dot_tn(d_score_b, one_head(query, second)),
                dot_tn(prob_b, d_mixed_here),
            )
            if d_query is None:
                d_query, d_key, d_value = parts
            else:
                d_query, d_key, d_value = d_query + parts[0], d_key + parts[1], d_value + parts[2]
        d_queries.append(d_query.astype(bf16))
        d_keys.append(d_key.astype(bf16))
        d_values_.append(d_value.astype(bf16))
    d_proj = jnp.concatenate(d_queries + d_keys + d_values_, 1)
    d_qkv = dot_tn(normed, d_proj)
    store_columns(grads_ref, 0, QKV_AT, d_qkv[:, : QKV_FIRST * LANES])
    store_columns(grads_ref, 1, QKV_REST_AT, d_qkv[:, QKV_FIRST * LANES :])
    d_normed = dot_nt(d_proj, w_qkv_ref[...])
    d_flat, d_gain_attn = norm_back(d_normed, gain_attn, unit, inverse)
    d_latent_ref[...] = (d_resid + d_flat).astype(bf16)

    rel = jnp.concatenate(rel_rows + [jnp.zeros((4, LANES), f32)], 0)
    rel_low = jnp.sum(jnp.where(low, rel, 0.0), 1, keepdims=True)
    rel_high = jnp.sum(jnp.where(low, 0.0, rel), 1, keepdims=True)
    grads_ref[0, REL_AT:HALF, :] = jnp.where(lane == 0, rel_low, jnp.where(lane == 1, rel_high, 0.0)).astype(bf16)
    gains = [g[:, k * LANES : (k + 1) * LANES] for g in (d_gain_attn, d_gain_mlp) for k in range(3)]
    grads_ref[1, GAIN_AT:HALF, :] = jnp.concatenate(gains + [jnp.zeros((HALF - GAIN_AT - 6, LANES), f32)], 0).astype(bf16)


def block(x, cot, gain_attn, w_qkv, rel_bias, w_out, gain_mlp, w_fc1, w_fc2, interpret=False):
    sides = jnp.stack([rel_bias[:, :6], rel_bias[:, 1:]], -1).reshape(HEADS * 42, 2)
    bias_rows = jnp.repeat(sides, SECTORS, 1)
    return pl.pallas_call(
        block_kernel,
        out_shape=(
            jax.ShapeDtypeStruct((CELLS, D), bf16),
            jax.ShapeDtypeStruct((CELLS, D), bf16),
            jax.ShapeDtypeStruct((2, HALF, LANES), bf16),
        ),
        compiler_params=pltpu.CompilerParams(vmem_limit_bytes=56 * 1024 * 1024),
        interpret=interpret,
    )(x, cot, gain_attn.reshape(1, D), w_qkv, bias_rows, w_out, gain_mlp.reshape(1, D), w_fc1, w_fc2)


def exchange(value, axes):
    return lax.all_to_all(value, axes, 0, 0)


def total(value):
    return jnp.sum(value.astype(f32), 0).astype(bf16)


def to_sibling(value):
    return lax.ppermute(value, "core", [(0, 1), (1, 0)])


def reduce_everywhere(grads):
    core = lax.axis_index("core")
    arrived = to_sibling(lax.dynamic_index_in_dim(grads, 1 - core, 0, False))
    kept = lax.dynamic_index_in_dim(grads, core, 0, False)
    here = (kept.astype(f32) + arrived.astype(f32)).astype(bf16)
    here = total(exchange(here.reshape(16, PIECE, LANES), PLANE))
    here = total(exchange(here.reshape(8, PART, LANES), "z"))
    here = exchange(jnp.broadcast_to(here, (8, PART, LANES)), "z").reshape(PIECE, LANES)
    here = exchange(jnp.broadcast_to(here, (16, PIECE, LANES)), PLANE).reshape(HALF, LANES)
    other = to_sibling(here)
    return jnp.where(core == 0, here, other), jnp.where(core == 0, other, here)


def beside(half, at, blocks, rows):
    taken = half[at : at + blocks * rows].reshape(blocks, rows, LANES)
    return jnp.transpose(taken, (1, 0, 2)).reshape(rows, blocks * LANES).astype(f32)


def per_device(latent, cotangent, gain_attn, w_qkv, rel_bias, w_out, gain_mlp, w_fc1, w_fc2):
    shape = latent.shape
    sent = jnp.stack([latent.reshape(CELLS, D), cotangent.reshape(CELLS, D)], 1)
    arrived = exchange(sent, AXES)
    out, d_latent, grads = block(
        arrived[:, 0], arrived[:, 1], gain_attn, w_qkv, rel_bias, w_out, gain_mlp, w_fc1, w_fc2
    )
    home = exchange(jnp.stack([out, d_latent], 1), AXES)
    first, second = reduce_everywhere(grads)
    d_qkv = jnp.concatenate(
        [beside(first, QKV_AT, QKV_FIRST, D), beside(second, QKV_REST_AT, 9 - QKV_FIRST, D)], 1
    )
    d_out = beside(second, OUT_AT, 3, D)
    d_fc1 = beside(first, FC1_AT, 12, D)
    d_fc2 = beside(second, FC2_AT, 3, FF)
    rel = first[REL_AT : REL_AT + HEADS * 42, :2].astype(f32).reshape(HEADS, 6, 7, 2)
    d_rel = jnp.pad(rel[..., 0], ((0, 0), (0, 1), (0, 0))) + jnp.pad(rel[..., 1], ((0, 0), (1, 0), (0, 0)))
    gains = second[GAIN_AT : GAIN_AT + 6].astype(f32).reshape(2, D)
    return home[:, 0].reshape(shape), home[:, 1].reshape(shape), d_qkv, d_out, d_fc1, d_fc2, d_rel, gains[0], gains[1]


def solution(mesh):
    split = Mesh(mesh.devices.reshape(2, 2, 2, 4, 8), AXES)
    cells = P(("y_lo", "core"), ("y_hi", "x", "z"), None)
    return jax.shard_map(
        per_device,
        mesh=split,
        in_specs=(cells, cells) + (P(),) * 7,
        out_specs=(cells, cells) + (P(),) * 7,
        check_vma=False,
    )
```

```python
import jax
import jax.numpy as jnp
from jax import lax
from jax.experimental import pallas as pl
from jax.experimental.pallas import tpu as pltpu
from jax.sharding import Mesh, PartitionSpec as P

HEADS = 6
HEAD = 64
D = 384
FF = 1536
BANDS = 4
SECTORS = 64
CELLS = BANDS * SECTORS
SCALE = HEAD ** (-0.5)
ABSENT = -1e30
AXES = ("y_lo", "core", "y_hi", "x", "z")
PLANE = ("y_lo", "y_hi", "x")

LANES = 128
PLACES = 16
DEPTH = 8
GRADS = 448
PART = GRADS // DEPTH
OWN = 48
PART_ROOM = 64
FC1_AT, QKV_AT = 0, 288
FC2_AT, OUT_AT, QKV_REST_AT = 0, 288, 360
SMALL_AT = 432
QKV_FIRST = 6

f32, bf16 = jnp.float32, jnp.bfloat16


def dot(a, b):
    return lax.dot_general(a, b, (((1,), (0,)), ((), ())), preferred_element_type=f32)


def dot_nt(a, b):
    return lax.dot_general(a, b, (((1,), (1,)), ((), ())), preferred_element_type=f32)


def dot_tn(a, b):
    return lax.dot_general(a, b, (((0,), (0,)), ((), ())), preferred_element_type=f32)


def norm(values):
    centred = values - jnp.mean(values, -1, keepdims=True)
    inverse = lax.rsqrt(jnp.mean(centred * centred, -1, keepdims=True) + 1e-05)
    return centred * inverse, inverse


def norm_back(d_normed, gain, unit, inverse):
    d_unit = d_normed * gain
    d_values = inverse * (
        d_unit
        - jnp.mean(d_unit, -1, keepdims=True)
        - unit * jnp.mean(d_unit * unit, -1, keepdims=True)
    )
    return d_values, jnp.sum(d_normed * unit, 0, keepdims=True)


def gelu_and_slope(x):
    root = 0.7978845608028654
    square = x * x
    t = jnp.tanh(root * x * (1.0 + 0.044715 * square))
    half = 0.5 * (1.0 + t)
    slope = half + (0.5 * root) * x * (1.0 - t * t) * (1.0 + 3.0 * 0.044715 * square)
    return x * half, slope


def store_columns(ref, half, at, values):
    rows = values.shape[0] // 8
    for block in range(values.shape[1] // LANES):
        here = values[:, block * LANES : (block + 1) * LANES].reshape(8, rows, LANES)
        first = at + block // 2 * rows
        start = block % 2 * 8
        ref[half, start : start + 8, first : first + rows, :] = here.astype(bf16)


def block_kernel(core_ref, x_ref, cot_ref, gain_attn_ref, w_qkv_ref, bias_ref, w_out_ref, gain_mlp_ref, w_fc1_ref, w_fc2_ref,
                 kept_ref, sent_ref, halves_ref):
    x = x_ref[...].astype(f32)
    gain_attn = gain_attn_ref[...]
    unit, inverse = norm(x)
    normed = (unit * gain_attn).astype(bf16)
    projected = dot(normed, w_qkv_ref[...]).astype(bf16)

    lane = lax.broadcasted_iota(jnp.int32, (1, LANES), 1)
    low = lane < HEAD
    apart = (
        lax.broadcasted_iota(jnp.int32, (SECTORS, LANES), 1)
        - lax.broadcasted_iota(jnp.int32, (SECTORS, LANES), 0)
    ) & (SECTORS - 1)

    def one_head(pair, second):
        return jnp.where(low, jnp.bfloat16(0), pair) if second else jnp.where(low, pair, jnp.bfloat16(0))

    def pair_of(array, part, pair):
        start = part * D + pair * LANES
        return array[:, start : start + LANES]

    probs, probs_b, mixed = [], [], []
    for pair in range(HEADS // 2):
        query, key, value = (pair_of(projected, part, pair) for part in range(3))
        total = None
        for second in range(2):
            head = 2 * pair + second
            tiles = []
            for first in range(6):
                tile = jnp.full((SECTORS, LANES), ABSENT, f32)
                for step in range(7):
                    row = bias_ref[(head * 6 + first) * 7 + step : (head * 6 + first) * 7 + step + 1, :]
                    tile = jnp.where(apart == (step - 3) % SECTORS, row, tile)
                tiles.append(tile)
            bias = jnp.concatenate(
                [jnp.concatenate([tiles[2 * side - band + 3] for band in range(BANDS)], 0) for side in range(2)], 1
            )
            score = dot_nt(one_head(query, second), key) * SCALE + bias
            weight = jnp.exp(score)
            prob = weight / jnp.sum(weight, -1, keepdims=True)
            prob_b = prob.astype(bf16)
            probs.append(prob)
            probs_b.append(prob_b)
            part = dot(prob_b, one_head(value, second))
            total = part if total is None else total + part
        mixed.append(total.astype(bf16))
    mixed = jnp.concatenate(mixed, 1)

    resid = x + dot(mixed, w_out_ref[...])
    gain_mlp = gain_mlp_ref[...]
    unit_two, inverse_two = norm(resid)
    normed_two = (unit_two * gain_mlp).astype(bf16)
    hidden = dot(normed_two, w_fc1_ref[...])
    active, slope = gelu_and_slope(hidden)
    active = active.astype(bf16)
    output = resid + dot(active, w_fc2_ref[...])

    cot = cot_ref[...]
    d_fc2 = dot_tn(active, cot)
    for block in range(3):
        here = d_fc2[:, block * LANES : (block + 1) * LANES].reshape(PLACES, FF // PLACES, LANES)
        halves_ref[1, :, FC2_AT + block * 96 : FC2_AT + block * 96 + 96, :] = here.astype(bf16)
    d_hidden = (dot_nt(cot, w_fc2_ref[...]) * slope).astype(bf16)
    store_columns(halves_ref, 0, FC1_AT, dot_tn(normed_two, d_hidden))
    d_normed_two = dot_nt(d_hidden, w_fc1_ref[...])
    d_values, d_gain_mlp = norm_back(d_normed_two, gain_mlp, unit_two, inverse_two)
    d_resid = cot.astype(f32) + d_values
    d_resid_b = d_resid.astype(bf16)
    d_out = dot_tn(mixed, d_resid_b)
    d_mixed = dot_nt(d_resid_b, w_out_ref[...]).astype(bf16)

    d_queries, d_keys, d_values_ = [], [], []
    rel_rows = []
    for pair in range(HEADS // 2):
        query, key, value = (pair_of(projected, part, pair) for part in range(3))
        d_mixed_pair = pair_of(d_mixed, 0, pair)
        d_query = d_key = d_value = None
        for second in range(2):
            head = 2 * pair + second
            prob, prob_b = probs[head], probs_b[head]
            d_mixed_here = one_head(d_mixed_pair, second)
            d_prob = dot_nt(d_mixed_here, value)
            d_score = prob * (d_prob - jnp.sum(prob * d_prob, -1, keepdims=True))
            sums = []
            for first in range(6):
                tile = None
                for band in range(BANDS):
                    for side in range(2):
                        if 2 * side - band + 3 == first:
                            here = d_score[band * SECTORS : (band + 1) * SECTORS, side * LANES : (side + 1) * LANES]
                            tile = here if tile is None else tile + here
                for step in range(7):
                    sums.append(jnp.sum(jnp.where(apart == (step - 3) % SECTORS, tile, 0.0), 0, keepdims=True))
            none = jnp.zeros((7, LANES), f32)
            sums = jnp.concatenate(sums, 0)
            taps = jnp.concatenate([jnp.where(low, sums, 0.0), none], 0) + jnp.concatenate(
                [none, jnp.where(low, 0.0, sums)], 0
            )
            taps = jnp.concatenate([taps, jnp.zeros((LANES - 49, LANES), f32)], 0)
            rel_rows.append(
                lax.dot_general(
                    jnp.ones((8, LANES), f32), taps, (((1,), (1,)), ((), ())),
                    precision=lax.Precision.HIGHEST, preferred_element_type=f32,
                )[:1]
            )
            d_score_b = (d_score * SCALE).astype(bf16)
            parts = (
                dot(d_score_b, one_head(key, second)),
                dot_tn(d_score_b, one_head(query, second)),
                dot_tn(prob_b, d_mixed_here),
            )
            if d_query is None:
                d_query, d_key, d_value = parts
            else:
                d_query, d_key, d_value = d_query + parts[0], d_key + parts[1], d_value + parts[2]
        d_queries.append(d_query.astype(bf16))
        d_keys.append(d_key.astype(bf16))
        d_values_.append(d_value.astype(bf16))
    d_proj = jnp.concatenate(d_queries + d_keys + d_values_, 1)
    d_qkv = dot_tn(normed, d_proj)
    store_columns(halves_ref, 0, QKV_AT, d_qkv[:, : QKV_FIRST * LANES])
    store_columns(halves_ref, 1, OUT_AT, jnp.concatenate([d_out, d_qkv[:, QKV_FIRST * LANES :]], 1))
    d_normed = dot_nt(d_proj, w_qkv_ref[...])
    d_flat, d_gain_attn = norm_back(d_normed, gain_attn, unit, inverse)
    d_latent = d_resid + d_flat

    gains = [g[:, k * LANES : (k + 1) * LANES] for g in (d_gain_attn, d_gain_mlp) for k in range(3)]
    small = jnp.concatenate(rel_rows + [jnp.zeros((2, LANES), f32)] + gains + [jnp.zeros((2, LANES), f32)], 0)
    halves_ref[0, 0, SMALL_AT:GRADS, :] = small.astype(bf16)
    halves_ref[0, 1:, SMALL_AT:GRADS, :] = jnp.zeros((PLACES - 1, GRADS - SMALL_AT, LANES), bf16)
    halves_ref[1, :, SMALL_AT:GRADS, :] = jnp.zeros((PLACES, GRADS - SMALL_AT, LANES), bf16)
    for band in range(BANDS):
        y_lo, core = band // 2, band % 2
        rows = slice(band * SECTORS, (band + 1) * SECTORS)
        for block in range(3):
            lanes = slice(block * LANES, (block + 1) * LANES)
            both = jnp.concatenate([a[rows, lanes].reshape(8, DEPTH, LANES) for a in (output, d_latent)], 1)
            at = GRADS + block * 16
            halves_ref[core, y_lo * 8 : y_lo * 8 + 8, at : at + 16, :] = both.astype(bf16)
    core = core_ref[0]
    kept_ref[...] = halves_ref[core]
    sent_ref[...] = halves_ref[1 - core]


def params():
    return pltpu.CompilerParams(vmem_limit_bytes=56 * 1024 * 1024)


SCALAR = pl.BlockSpec(memory_space=pltpu.SMEM)
WHOLE = pl.BlockSpec(memory_space=pltpu.VMEM)


def block(core, x, cot, gain_attn, w_qkv, rel_bias, w_out, gain_mlp, w_fc1, w_fc2, interpret=False):
    sides = jnp.stack([rel_bias[:, :6], rel_bias[:, 1:]], -1).reshape(HEADS * 42, 2)
    bias_rows = jnp.repeat(sides, SECTORS, 1)
    half = jax.ShapeDtypeStruct((PLACES, GRADS + OWN, LANES), bf16)
    return pl.pallas_call(
        block_kernel,
        out_shape=(half, half),
        in_specs=[SCALAR] + [WHOLE] * 9,
        out_specs=(WHOLE, WHOLE),
        scratch_shapes=[pltpu.VMEM((2, PLACES, GRADS + OWN, LANES), bf16)],
        compiler_params=params(),
        interpret=interpret,
    )(core, x, cot, gain_attn.reshape(1, D), w_qkv, bias_rows, w_out, gain_mlp.reshape(1, D), w_fc1, w_fc2)


def merge_kernel(core_ref, kept_ref, arrived_ref, out_ref):
    total = kept_ref[:, :GRADS, :].astype(f32) + arrived_ref[:, :GRADS, :].astype(f32)
    out_ref[:, :GRADS, :] = total.astype(bf16)

    def cells(first, second):
        out_ref[:, GRADS : GRADS + OWN, :] = first[:, GRADS:, :]
        out_ref[:, GRADS + OWN :, :] = second[:, GRADS:, :]

    @pl.when(core_ref[0] == 0)
    def _():
        cells(kept_ref, arrived_ref)

    @pl.when(core_ref[0] != 0)
    def _():
        cells(arrived_ref, kept_ref)


def merge(core, kept, arrived, interpret=False):
    return pl.pallas_call(
        merge_kernel,
        out_shape=jax.ShapeDtypeStruct((PLACES, GRADS + 2 * OWN, LANES), bf16),
        in_specs=[SCALAR, WHOLE, WHOLE],
        out_specs=WHOLE,
        compiler_params=params(),
        interpret=interpret,
    )(core, kept, arrived)


def plane_kernel(arrived_ref, out_ref):
    total = arrived_ref[0, :GRADS, :].astype(f32)
    for place in range(1, PLACES):
        total = total + arrived_ref[place, :GRADS, :].astype(f32)
    room = jnp.zeros((DEPTH, PART_ROOM - PART, LANES), f32)
    out_ref[:, :PART_ROOM, :] = jnp.concatenate([total.reshape(DEPTH, PART, LANES), room], 1).astype(bf16)
    count = 2 * PLACES * 2 * DEPTH
    blocks = []
    for block in range(3):
        at = GRADS + block * 16
        blocks.append(
            jnp.concatenate([arrived_ref[:, at + c * OWN : at + c * OWN + 16, :].reshape(256, LANES) for c in range(2)], 0)
        )
    rows = jnp.concatenate(blocks, 1)
    to = lax.broadcasted_iota(jnp.int32, (count, count), 0)
    source = ((to & 1) << 8) | (((to >> 1) & 15) << 4) | (((to >> 5) & 1) << 3) | (to >> 6)
    chosen = jnp.where(lax.broadcasted_iota(jnp.int32, (count, count), 1) == source, 1.0, 0.0).astype(bf16)
    moved = dot(chosen, rows).astype(bf16).reshape(DEPTH, 2, 32, 3 * LANES)
    for array in range(2):
        for block in range(3):
            at = PART_ROOM + (array * 3 + block) * 32
            out_ref[:, at : at + 32, :] = moved[:, array, :, block * LANES : (block + 1) * LANES]


def plane(arrived, interpret=False):
    return pl.pallas_call(
        plane_kernel,
        out_shape=jax.ShapeDtypeStruct((DEPTH, PART_ROOM + 192, LANES), bf16),
        in_specs=[WHOLE],
        out_specs=WHOLE,
        compiler_params=params(),
        interpret=interpret,
    )(arrived)


def depth_kernel(arrived_ref, part_ref, output_ref, d_latent_ref):
    total = jnp.sum(arrived_ref[:, :PART_ROOM, :].astype(f32), 0)[:PART]
    part_ref[...] = jnp.broadcast_to(total[None], (DEPTH, PART, LANES)).astype(bf16)
    for array, ref in enumerate((output_ref, d_latent_ref)):
        for block in range(3):
            at = PART_ROOM + (array * 3 + block) * 32
            ref[:, block * LANES : (block + 1) * LANES] = arrived_ref[:, at : at + 32, :].reshape(CELLS, LANES)


def depth(arrived, interpret=False):
    cells = jax.ShapeDtypeStruct((CELLS, D), bf16)
    return pl.pallas_call(
        depth_kernel,
        out_shape=(jax.ShapeDtypeStruct((DEPTH, PART, LANES), bf16), cells, cells),
        in_specs=[WHOLE],
        out_specs=(WHOLE, WHOLE, WHOLE),
        compiler_params=params(),
        interpret=interpret,
    )(arrived)


def assemble_kernel(core_ref, here_ref, other_ref, d_qkv_ref, d_out_ref, d_fc1_ref, d_fc2_ref, small_ref):
    def columns(half, at, block, rows):
        first = at + block // 2 * rows
        start = block % 2 * 8
        return half[start : start + 8, first : first + rows, :].astype(f32).reshape(8 * rows, LANES)

    def lanes(block):
        return slice(block * LANES, (block + 1) * LANES)

    def write(first, second):
        for block in range(12):
            d_fc1_ref[:, lanes(block)] = columns(first, FC1_AT, block, 48)
        for block in range(3):
            at = FC2_AT + block * 96
            d_fc2_ref[:, lanes(block)] = second[:, at : at + 96, :].astype(f32).reshape(FF, LANES)
        for block in range(9):
            if block < QKV_FIRST:
                d_qkv_ref[:, lanes(block)] = columns(first, QKV_AT, block, 48)
            else:
                d_qkv_ref[:, lanes(block)] = columns(second, OUT_AT, block - QKV_FIRST + 3, 48)
        for block in range(3):
            d_out_ref[:, lanes(block)] = columns(second, OUT_AT, block, 48)
        small_ref[...] = first[0, SMALL_AT:GRADS, :].astype(f32)

    @pl.when(core_ref[0] == 0)
    def _():
        write(here_ref, other_ref)

    @pl.when(core_ref[0] != 0)
    def _():
        write(other_ref, here_ref)


def assemble(core, here, other, interpret=False):
    shapes = ((D, 3 * D), (D, D), (D, FF), (FF, D), (16, LANES))
    return pl.pallas_call(
        assemble_kernel,
        out_shape=tuple(jax.ShapeDtypeStruct(s, f32) for s in shapes),
        in_specs=[SCALAR, WHOLE, WHOLE],
        out_specs=(WHOLE,) * 5,
        compiler_params=params(),
        interpret=interpret,
    )(core, here, other)


def exchange(value, axes):
    return lax.all_to_all(value, axes, 0, 0)


def to_sibling(value):
    return lax.ppermute(value, "core", [(0, 1), (1, 0)])


def per_device(latent, cotangent, gain_attn, w_qkv, rel_bias, w_out, gain_mlp, w_fc1, w_fc2):
    shape = latent.shape
    core = lax.axis_index("core").reshape(1)
    both = jnp.stack([latent.reshape(CELLS, D), cotangent.reshape(CELLS, D)], 1).reshape(DEPTH, 2, 2, 4, 2, 2, D)
    sent = jnp.transpose(both, (1, 4, 2, 3, 0, 5, 6)).reshape(CELLS, 2, D)
    arrived = exchange(sent, AXES)
    kept, sent = block(core, arrived[:, 0], arrived[:, 1], gain_attn, w_qkv, rel_bias, w_out, gain_mlp, w_fc1, w_fc2)
    merged = merge(core, kept, to_sibling(sent))
    part, output, d_latent = depth(exchange(plane(exchange(merged, PLANE)), "z"))
    piece = exchange(part, "z").reshape(GRADS, LANES)
    here = exchange(jnp.broadcast_to(piece, (PLACES, GRADS, LANES)), PLANE)
    d_qkv, d_out, d_fc1, d_fc2, small = assemble(core, here, to_sibling(here))
    d_rel = small[:HEADS, :49].reshape(HEADS, 7, 7)
    gains = small[8:14].reshape(2, D)
    return output.reshape(shape), d_latent.reshape(shape), d_qkv, d_out, d_fc1, d_fc2, d_rel, gains[0], gains[1]


def solution(mesh):
    split = Mesh(mesh.devices.reshape(2, 2, 2, 4, 8), AXES)
    cells = P(("y_lo", "core"), ("y_hi", "x", "z"), None)
    return jax.shard_map(
        per_device,
        mesh=split,
        in_specs=(cells, cells) + (P(),) * 7,
        out_specs=(cells, cells) + (P(),) * 7,
        check_vma=False,
    )
```

```python
import jax
import jax.numpy as jnp
from jax import lax
from jax.experimental import pallas as pl
from jax.experimental.pallas import tpu as pltpu
from jax.sharding import Mesh, PartitionSpec as P

HEADS = 6
HEAD = 64
D = 384
FF = 1536
BANDS = 4
SECTORS = 64
CELLS = BANDS * SECTORS
SCALE = HEAD ** (-0.5)
ABSENT = -1e30
AXES = ("y_lo", "core", "y_hi", "x", "z")
PLANE = ("y_lo", "y_hi", "x")

LANES = 128
PLACES = 16
DEPTH = 8
GRADS = 448
PART = GRADS // DEPTH
OWN = 48
PART_ROOM = 64
FC1_AT, QKV_AT = 0, 288
FC2_AT, OUT_AT, QKV_REST_AT = 0, 288, 360
SMALL_AT = 432
QKV_FIRST = 6

f32, bf16 = jnp.float32, jnp.bfloat16


def dot(a, b):
    return lax.dot_general(a, b, (((1,), (0,)), ((), ())), preferred_element_type=f32)


def dot_nt(a, b):
    return lax.dot_general(a, b, (((1,), (1,)), ((), ())), preferred_element_type=f32)


def dot_tn(a, b):
    return lax.dot_general(a, b, (((0,), (0,)), ((), ())), preferred_element_type=f32)


def norm(values):
    centred = values - jnp.mean(values, -1, keepdims=True)
    inverse = lax.rsqrt(jnp.mean(centred * centred, -1, keepdims=True) + 1e-05)
    return centred * inverse, inverse


def norm_back(d_normed, gain, unit, inverse):
    d_unit = d_normed * gain
    d_values = inverse * (
        d_unit
        - jnp.mean(d_unit, -1, keepdims=True)
        - unit * jnp.mean(d_unit * unit, -1, keepdims=True)
    )
    return d_values, jnp.sum(d_normed * unit, 0, keepdims=True)


def gelu_and_slope(x):
    root = 0.7978845608028654
    square = x * x
    t = jnp.tanh(root * x * (1.0 + 0.044715 * square))
    half = 0.5 * (1.0 + t)
    slope = half + (0.5 * root) * x * (1.0 - t * t) * (1.0 + 3.0 * 0.044715 * square)
    return x * half, slope


def store_columns(ref, half, at, values):
    rows = values.shape[0] // 8
    for block in range(values.shape[1] // LANES):
        here = values[:, block * LANES : (block + 1) * LANES].reshape(8, rows, LANES)
        first = at + block // 2 * rows
        start = block % 2 * 8
        ref[half, start : start + 8, first : first + rows, :] = here.astype(bf16)


def block_kernel(core_ref, x_ref, cot_ref, gain_attn_ref, w_qkv_ref, bias_ref, w_out_ref, gain_mlp_ref, w_fc1_ref, w_fc2_ref,
                 kept_ref, sent_ref, halves_ref):
    x = x_ref[...].astype(f32)
    gain_attn = gain_attn_ref[...]
    unit, inverse = norm(x)
    normed = (unit * gain_attn).astype(bf16)
    projected = dot(normed, w_qkv_ref[...]).astype(bf16)

    lane = lax.broadcasted_iota(jnp.int32, (1, LANES), 1)
    low = lane < HEAD
    apart = (
        lax.broadcasted_iota(jnp.int32, (SECTORS, LANES), 1)
        - lax.broadcasted_iota(jnp.int32, (SECTORS, LANES), 0)
    ) & (SECTORS - 1)

    def one_head(pair, second):
        return jnp.where(low, jnp.bfloat16(0), pair) if second else jnp.where(low, pair, jnp.bfloat16(0))

    def pair_of(array, part, pair):
        start = part * D + pair * LANES
        return array[:, start : start + LANES]

    probs, probs_b, mixed = [], [], []
    for pair in range(HEADS // 2):
        query, key, value = (pair_of(projected, part, pair) for part in range(3))
        total = None
        for second in range(2):
            head = 2 * pair + second
            tiles = []
            for first in range(6):
                tile = jnp.full((SECTORS, LANES), ABSENT, f32)
                for step in range(7):
                    row = bias_ref[(head * 6 + first) * 7 + step : (head * 6 + first) * 7 + step + 1, :]
                    tile = jnp.where(apart == (step - 3) % SECTORS, row, tile)
                tiles.append(tile)
            bias = jnp.concatenate(
                [jnp.concatenate([tiles[2 * side - band + 3] for band in range(BANDS)], 0) for side in range(2)], 1
            )
            score = dot_nt(one_head(query, second), key) * SCALE + bias
            weight = jnp.exp(score)
            prob = weight * (1.0 / jnp.sum(weight, -1, keepdims=True))
            prob_b = prob.astype(bf16)
            probs.append(prob)
            probs_b.append(prob_b)
            part = dot(prob_b, one_head(value, second))
            total = part if total is None else total + part
        mixed.append(total.astype(bf16))
    mixed = jnp.concatenate(mixed, 1)

    resid = x + dot(mixed, w_out_ref[...])
    gain_mlp = gain_mlp_ref[...]
    unit_two, inverse_two = norm(resid)
    normed_two = (unit_two * gain_mlp).astype(bf16)
    hidden = dot(normed_two, w_fc1_ref[...])
    active, slope = gelu_and_slope(hidden)
    active = active.astype(bf16)
    output = resid + dot(active, w_fc2_ref[...])

    cot = cot_ref[...]
    d_fc2 = dot_tn(active, cot)
    for block in range(3):
        here = d_fc2[:, block * LANES : (block + 1) * LANES].reshape(PLACES, FF // PLACES, LANES)
        halves_ref[1, :, FC2_AT + block * 96 : FC2_AT + block * 96 + 96, :] = here.astype(bf16)
    d_hidden = (dot_nt(cot, w_fc2_ref[...]) * slope).astype(bf16)
    store_columns(halves_ref, 0, FC1_AT, dot_tn(normed_two, d_hidden))
    d_normed_two = dot_nt(d_hidden, w_fc1_ref[...])
    d_values, d_gain_mlp = norm_back(d_normed_two, gain_mlp, unit_two, inverse_two)
    d_resid = cot.astype(f32) + d_values
    d_resid_b = d_resid.astype(bf16)
    d_out = dot_tn(mixed, d_resid_b)
    d_mixed = dot_nt(d_resid_b, w_out_ref[...]).astype(bf16)

    d_queries, d_keys, d_values_ = [], [], []
    rel_rows = []
    for pair in range(HEADS // 2):
        query, key, value = (pair_of(projected, part, pair) for part in range(3))
        d_mixed_pair = pair_of(d_mixed, 0, pair)
        d_query = d_key = d_value = None
        for second in range(2):
            head = 2 * pair + second
            prob, prob_b = probs[head], probs_b[head]
            d_mixed_here = one_head(d_mixed_pair, second)
            d_prob = dot_nt(d_mixed_here, value)
            d_score = prob * (d_prob - jnp.sum(prob * d_prob, -1, keepdims=True))
            sums = []
            for first in range(6):
                tile = None
                for band in range(BANDS):
                    for side in range(2):
                        if 2 * side - band + 3 == first:
                            here = d_score[band * SECTORS : (band + 1) * SECTORS, side * LANES : (side + 1) * LANES]
                            tile = here if tile is None else tile + here
                for step in range(7):
                    sums.append(jnp.sum(jnp.where(apart == (step - 3) % SECTORS, tile, 0.0), 0, keepdims=True))
            none = jnp.zeros((7, LANES), f32)
            sums = jnp.concatenate(sums, 0)
            taps = jnp.concatenate([jnp.where(low, sums, 0.0), none], 0) + jnp.concatenate(
                [none, jnp.where(low, 0.0, sums)], 0
            )
            taps = jnp.concatenate([taps, jnp.zeros((LANES - 49, LANES), f32)], 0)
            rel_rows.append(
                lax.dot_general(
                    jnp.ones((8, LANES), f32), taps, (((1,), (1,)), ((), ())),
                    precision=lax.Precision.HIGHEST, preferred_element_type=f32,
                )[:1]
            )
            d_score_b = (d_score * SCALE).astype(bf16)
            parts = (
                dot(d_score_b, one_head(key, second)),
                dot_tn(d_score_b, one_head(query, second)),
                dot_tn(prob_b, d_mixed_here),
            )
            if d_query is None:
                d_query, d_key, d_value = parts
            else:
                d_query, d_key, d_value = d_query + parts[0], d_key + parts[1], d_value + parts[2]
        d_queries.append(d_query.astype(bf16))
        d_keys.append(d_key.astype(bf16))
        d_values_.append(d_value.astype(bf16))
    d_proj = jnp.concatenate(d_queries + d_keys + d_values_, 1)
    d_qkv = dot_tn(normed, d_proj)
    store_columns(halves_ref, 0, QKV_AT, d_qkv[:, : QKV_FIRST * LANES])
    store_columns(halves_ref, 1, OUT_AT, jnp.concatenate([d_out, d_qkv[:, QKV_FIRST * LANES :]], 1))
    d_normed = dot_nt(d_proj, w_qkv_ref[...])
    d_flat, d_gain_attn = norm_back(d_normed, gain_attn, unit, inverse)
    d_latent = d_resid + d_flat

    gains = [g[:, k * LANES : (k + 1) * LANES] for g in (d_gain_attn, d_gain_mlp) for k in range(3)]
    small = jnp.concatenate(rel_rows + [jnp.zeros((2, LANES), f32)] + gains + [jnp.zeros((2, LANES), f32)], 0)
    halves_ref[0, 0, SMALL_AT:GRADS, :] = small.astype(bf16)
    halves_ref[0, 1:, SMALL_AT:GRADS, :] = jnp.zeros((PLACES - 1, GRADS - SMALL_AT, LANES), bf16)
    halves_ref[1, :, SMALL_AT:GRADS, :] = jnp.zeros((PLACES, GRADS - SMALL_AT, LANES), bf16)
    for band in range(BANDS):
        y_lo, core = band // 2, band % 2
        rows = slice(band * SECTORS, (band + 1) * SECTORS)
        for block in range(3):
            lanes = slice(block * LANES, (block + 1) * LANES)
            both = jnp.concatenate([a[rows, lanes].reshape(8, DEPTH, LANES) for a in (output, d_latent)], 1)
            at = GRADS + block * 16
            halves_ref[core, y_lo * 8 : y_lo * 8 + 8, at : at + 16, :] = both.astype(bf16)
    core = core_ref[0]
    kept_ref[...] = halves_ref[core]
    sent_ref[...] = halves_ref[1 - core]


SCALAR = pl.BlockSpec(memory_space=pltpu.SMEM)
WHOLE = pl.BlockSpec(memory_space=pltpu.VMEM)


def call(kernel, outs, operands, interpret, room=16, scalars=0, scratch=()):
    shapes = tuple((pltpu.VMEM if near and not interpret else jax.ShapeDtypeStruct)(s, t) for s, t, near in outs)
    if not interpret:
        operands = operands[:scalars] + tuple(pltpu.with_memory_space_constraint(o, pltpu.VMEM) for o in operands[scalars:])
    return pl.pallas_call(
        kernel,
        out_shape=shapes,
        in_specs=[SCALAR] * scalars + [WHOLE] * (len(operands) - scalars),
        out_specs=(WHOLE,) * len(outs),
        scratch_shapes=scratch,
        compiler_params=pltpu.CompilerParams(vmem_limit_bytes=room * 1024 * 1024),
        interpret=interpret,
    )(*operands)


def block(core, x, cot, gain_attn, w_qkv, rel_bias, w_out, gain_mlp, w_fc1, w_fc2, interpret=False):
    sides = jnp.stack([rel_bias[:, :6], rel_bias[:, 1:]], -1).reshape(HEADS * 42, 2)
    bias_rows = jnp.repeat(sides, SECTORS, 1)
    half = (PLACES, GRADS + OWN, LANES)
    return call(
        block_kernel,
        ((half, bf16, True), (half, bf16, True)),
        (core, x, cot, gain_attn.reshape(1, D), w_qkv, bias_rows, w_out, gain_mlp.reshape(1, D), w_fc1, w_fc2),
        interpret,
        room=32,
        scalars=1,
        scratch=[pltpu.VMEM((2, *half), bf16)],
    )


def merge_kernel(core_ref, kept_ref, arrived_ref, out_ref):
    total = kept_ref[:, :GRADS, :].astype(f32) + arrived_ref[:, :GRADS, :].astype(f32)
    out_ref[:, :GRADS, :] = total.astype(bf16)

    def cells(first, second):
        out_ref[:, GRADS : GRADS + OWN, :] = first[:, GRADS:, :]
        out_ref[:, GRADS + OWN :, :] = second[:, GRADS:, :]

    @pl.when(core_ref[0] == 0)
    def _():
        cells(kept_ref, arrived_ref)

    @pl.when(core_ref[0] != 0)
    def _():
        cells(arrived_ref, kept_ref)


def merge(core, kept, arrived, interpret=False):
    out = ((PLACES, GRADS + 2 * OWN, LANES), bf16, True)
    return call(merge_kernel, (out,), (core, kept, arrived), interpret, scalars=1)[0]


def plane_kernel(arrived_ref, out_ref):
    total = arrived_ref[0, :GRADS, :].astype(f32)
    for place in range(1, PLACES):
        total = total + arrived_ref[place, :GRADS, :].astype(f32)
    room = jnp.zeros((DEPTH, PART_ROOM - PART, LANES), f32)
    out_ref[:, :PART_ROOM, :] = jnp.concatenate([total.reshape(DEPTH, PART, LANES), room], 1).astype(bf16)
    count = 2 * PLACES * 2 * DEPTH
    blocks = []
    for block in range(3):
        at = GRADS + block * 16
        blocks.append(
            jnp.concatenate([arrived_ref[:, at + c * OWN : at + c * OWN + 16, :].reshape(256, LANES) for c in range(2)], 0)
        )
    rows = jnp.concatenate(blocks, 1)
    to = lax.broadcasted_iota(jnp.int32, (count, count), 0)
    source = ((to & 1) << 8) | (((to >> 1) & 15) << 4) | (((to >> 5) & 1) << 3) | (to >> 6)
    chosen = jnp.where(lax.broadcasted_iota(jnp.int32, (count, count), 1) == source, 1.0, 0.0).astype(bf16)
    moved = dot(chosen, rows).astype(bf16).reshape(DEPTH, 2, 32, 3 * LANES)
    for array in range(2):
        for block in range(3):
            at = PART_ROOM + (array * 3 + block) * 32
            out_ref[:, at : at + 32, :] = moved[:, array, :, block * LANES : (block + 1) * LANES]


def plane(arrived, interpret=False):
    return call(plane_kernel, (((DEPTH, PART_ROOM + 192, LANES), bf16, True),), (arrived,), interpret)[0]


def depth_kernel(arrived_ref, part_ref, output_ref, d_latent_ref):
    total = jnp.sum(arrived_ref[:, :PART_ROOM, :].astype(f32), 0)[:PART]
    part_ref[...] = jnp.broadcast_to(total[None], (DEPTH, PART, LANES)).astype(bf16)
    to = lax.broadcasted_iota(jnp.int32, (CELLS, CELLS), 0)
    source = ((to & 7) << 5) | ((to >> 7) << 4) | (((to >> 3) & 7) << 1) | ((to >> 6) & 1)
    chosen = jnp.where(lax.broadcasted_iota(jnp.int32, (CELLS, CELLS), 1) == source, 1.0, 0.0).astype(bf16)
    for array, ref in enumerate((output_ref, d_latent_ref)):
        starts = [PART_ROOM + (array * 3 + block) * 32 for block in range(3)]
        rows = jnp.concatenate([arrived_ref[:, at : at + 32, :].reshape(CELLS, LANES) for at in starts], 1)
        ref[...] = dot(chosen, rows).astype(bf16)


def depth(arrived, interpret=False):
    cells = ((CELLS, D), bf16, False)
    return call(depth_kernel, (((DEPTH, PART, LANES), bf16, True), cells, cells), (arrived,), interpret)


def assemble_kernel(core_ref, here_ref, other_ref, d_qkv_ref, d_out_ref, d_fc1_ref, d_fc2_ref,
                    d_rel_ref, d_gain_attn_ref, d_gain_mlp_ref):
    def columns(half, at, block, rows):
        first = at + block // 2 * rows
        start = block % 2 * 8
        return half[start : start + 8, first : first + rows, :].astype(f32).reshape(8 * rows, LANES)

    def lanes(block):
        return slice(block * LANES, (block + 1) * LANES)

    def write(first, second):
        for block in range(12):
            d_fc1_ref[:, lanes(block)] = columns(first, FC1_AT, block, 48)
        for block in range(3):
            at = FC2_AT + block * 96
            d_fc2_ref[:, lanes(block)] = second[:, at : at + 96, :].astype(f32).reshape(FF, LANES)
        for block in range(9):
            if block < QKV_FIRST:
                d_qkv_ref[:, lanes(block)] = columns(first, QKV_AT, block, 48)
            else:
                d_qkv_ref[:, lanes(block)] = columns(second, OUT_AT, block - QKV_FIRST + 3, 48)
        for block in range(3):
            d_out_ref[:, lanes(block)] = columns(second, OUT_AT, block, 48)
        small = first[0, SMALL_AT:GRADS, :].astype(f32)
        for step in range(7):
            d_rel_ref[:, step, :] = pltpu.roll(small, (LANES - 7 * step) % LANES, 1)[:HEADS, :7]
        for block in range(3):
            d_gain_attn_ref[lanes(block)] = small[8 + block]
            d_gain_mlp_ref[lanes(block)] = small[11 + block]

    @pl.when(core_ref[0] == 0)
    def _():
        write(here_ref, other_ref)

    @pl.when(core_ref[0] != 0)
    def _():
        write(other_ref, here_ref)


def assemble(core, here, other, interpret=False):
    shapes = ((D, 3 * D), (D, D), (D, FF), (FF, D), (HEADS, 7, 7), (D,), (D,))
    return call(assemble_kernel, tuple((s, f32, False) for s in shapes), (core, here, other), interpret, scalars=1)


def exchange(value, axes):
    return lax.all_to_all(value, axes, 0, 0)


def to_sibling(value):
    return lax.ppermute(value, "core", [(0, 1), (1, 0)])


def per_device(latent, cotangent, gain_attn, w_qkv, rel_bias, w_out, gain_mlp, w_fc1, w_fc2):
    shape = latent.shape
    core = lax.axis_index("core").reshape(1)
    arrived = exchange(jnp.stack([latent.reshape(CELLS, D), cotangent.reshape(CELLS, D)], 1), AXES)
    kept, sent = block(core, arrived[:, 0], arrived[:, 1], gain_attn, w_qkv, rel_bias, w_out, gain_mlp, w_fc1, w_fc2)
    merged = merge(core, kept, to_sibling(sent))
    part, output, d_latent = depth(exchange(plane(exchange(merged, PLANE)), "z"))
    piece = exchange(part, "z").reshape(GRADS, LANES)
    here = exchange(jnp.broadcast_to(piece, (PLACES, GRADS, LANES)), PLANE)
    return (output.reshape(shape), d_latent.reshape(shape)) + assemble(core, here, to_sibling(here))


def solution(mesh):
    split = Mesh(mesh.devices.reshape(2, 2, 2, 4, 8), AXES)
    cells = P(("y_lo", "core"), ("y_hi", "x", "z"), None)
    return jax.shard_map(
        per_device,
        mesh=split,
        in_specs=(cells, cells) + (P(),) * 7,
        out_specs=(cells, cells) + (P(),) * 7,
        check_vma=False,
    )
```

```python
import jax
import jax.numpy as jnp
from jax import lax
from jax.experimental import pallas as pl
from jax.experimental.pallas import tpu as pltpu
from jax.sharding import Mesh, PartitionSpec as P

HEADS = 6
HEAD = 64
D = 384
FF = 1536
BANDS = 4
SECTORS = 64
CELLS = BANDS * SECTORS
SCALE = HEAD ** (-0.5)
ABSENT = -1e30
AXES = ("y_lo", "core", "y_hi", "x", "z")
PLANE = ("y_lo", "y_hi", "x")

LANES = 128
PLACES = 16
DEPTH = 8
GRADS = 448
PART = GRADS // DEPTH
OWN = 48
PART_ROOM = 64
FC1_AT, QKV_AT = 0, 288
FC2_AT, OUT_AT, QKV_REST_AT = 0, 288, 360
SMALL_AT = 432
QKV_FIRST = 6

f32, bf16 = jnp.float32, jnp.bfloat16


def dot(a, b):
    return lax.dot_general(a, b, (((1,), (0,)), ((), ())), preferred_element_type=f32)


def dot_nt(a, b):
    return lax.dot_general(a, b, (((1,), (1,)), ((), ())), preferred_element_type=f32)


def dot_tn(a, b):
    return lax.dot_general(a, b, (((0,), (0,)), ((), ())), preferred_element_type=f32)


def norm(values):
    centred = values - jnp.mean(values, -1, keepdims=True)
    inverse = lax.rsqrt(jnp.mean(centred * centred, -1, keepdims=True) + 1e-05)
    return centred * inverse, inverse


def norm_back(d_normed, gain, unit, inverse):
    d_unit = d_normed * gain
    d_values = inverse * (
        d_unit
        - jnp.mean(d_unit, -1, keepdims=True)
        - unit * jnp.mean(d_unit * unit, -1, keepdims=True)
    )
    return d_values, jnp.sum(d_normed * unit, 0, keepdims=True)


def gelu_and_slope(x):
    root = 0.7978845608028654
    square = x * x
    t = jnp.tanh(root * x * (1.0 + 0.044715 * square))
    half = 0.5 * (1.0 + t)
    slope = half + (0.5 * root) * x * (1.0 - t * t) * (1.0 + 3.0 * 0.044715 * square)
    return x * half, slope


def store_columns(ref, half, at, values):
    rows = values.shape[0] // 8
    for block in range(values.shape[1] // LANES):
        here = values[:, block * LANES : (block + 1) * LANES].reshape(8, rows, LANES)
        first = at + block // 2 * rows
        start = block % 2 * 8
        ref[half, start : start + 8, first : first + rows, :] = here.astype(bf16)


def bits(number, low, count):
    return (number >> low) & ((1 << count) - 1)


def reorder(rows, source):
    count = rows.shape[0]
    to = lax.broadcasted_iota(jnp.int32, (count, count), 0)
    chosen = jnp.where(lax.broadcasted_iota(jnp.int32, (count, count), 1) == source(to), 1.0, 0.0).astype(bf16)
    return dot(chosen, rows)


def pack_kernel(latent_ref, cot_ref, out_ref):
    for start in range(0, CELLS, 128):
        parts = [ref[start // 16 : start // 16 + 8].reshape(128, D) for ref in (latent_ref, cot_ref)]
        rows = reorder(jnp.concatenate(parts, 0), lambda to: bits(to, 0, 1) << 7 | to >> 1)
        out_ref[start : start + 128] = rows.astype(bf16).reshape(128, 2, D)


def pack(latent, cot, interpret=False):
    return call(pack_kernel, (((CELLS, 2, D), bf16, True),), (latent, cot), interpret, near=False)[0]


def fetch_kernel(*refs):
    count = len(refs) // 2
    sems = refs[-1]
    copies = [pltpu.make_async_copy(refs[i], refs[count + i], sems.at[i]) for i in range(count)]
    for copy in copies:
        copy.start()
    for copy in copies:
        copy.wait()


def fetch(*arrays):
    return pl.pallas_call(
        fetch_kernel,
        out_shape=tuple(pltpu.VMEM(a.shape, a.dtype) for a in arrays),
        in_specs=[pl.BlockSpec(memory_space=pltpu.HBM)] * len(arrays),
        out_specs=(WHOLE,) * len(arrays),
        scratch_shapes=[pltpu.SemaphoreType.DMA((len(arrays),))],
        compiler_params=pltpu.CompilerParams(vmem_limit_bytes=1024 * 1024),
    )(*(pltpu.with_memory_space_constraint(a, pltpu.HBM) for a in arrays))


def gain_row(ref):
    return jnp.concatenate([ref[lanes(block)].reshape(1, LANES) for block in range(3)], 1)


def block_kernel(core_ref, both_ref, gain_attn_ref, w_qkv_ref, bias_ref, w_out_ref, gain_mlp_ref, w_fc1_ref, w_fc2_far_ref,
                 kept_ref, sent_ref, halves_ref, w_fc2_ref, sem):
    w_fc2_copy = pltpu.make_async_copy(w_fc2_far_ref, w_fc2_ref, sem)
    w_fc2_copy.start()
    groups = [both_ref[start : start + 128].reshape(256, D) for start in range(0, CELLS, 128)]
    groups = [reorder(group, lambda to: bits(to, 0, 7) << 1 | to >> 7) for group in groups]
    x = jnp.concatenate([group[:128] for group in groups], 0)
    gain_attn = gain_row(gain_attn_ref)
    unit, inverse = norm(x)
    normed = (unit * gain_attn).astype(bf16)
    projected = dot(normed, w_qkv_ref[...]).astype(bf16)

    lane = lax.broadcasted_iota(jnp.int32, (1, LANES), 1)
    low = lane < HEAD
    apart = (
        lax.broadcasted_iota(jnp.int32, (SECTORS, LANES), 1)
        - lax.broadcasted_iota(jnp.int32, (SECTORS, LANES), 0)
    ) & (SECTORS - 1)

    same = lax.broadcasted_iota(jnp.int32, (7, 7), 0) == lax.broadcasted_iota(jnp.int32, (7, 7), 1)
    bias_rows = []
    for head in range(HEADS):
        table = bias_ref[head]
        columns = [jnp.sum(jnp.where(same, table[band : band + 1], 0.0), 1, keepdims=True) for band in range(7)]
        bias_rows.append([jnp.where(low, columns[first], columns[first + 1]) for first in range(6)])

    def one_head(pair, second):
        return jnp.where(low, jnp.bfloat16(0), pair) if second else jnp.where(low, pair, jnp.bfloat16(0))

    def pair_of(array, part, pair):
        start = part * D + pair * LANES
        return array[:, start : start + LANES]

    probs, probs_b, mixed = [], [], []
    for pair in range(HEADS // 2):
        query, key, value = (pair_of(projected, part, pair) for part in range(3))
        query = query * jnp.bfloat16(SCALE)
        total = None
        for second in range(2):
            head = 2 * pair + second
            tiles = []
            for first in range(6):
                tile = jnp.full((SECTORS, LANES), ABSENT, f32)
                for step in range(7):
                    row = bias_rows[head][first][step : step + 1]
                    tile = jnp.where(apart == (step - 3) % SECTORS, row, tile)
                tiles.append(tile)
            bias = jnp.concatenate(
                [jnp.concatenate([tiles[2 * side - band + 3] for band in range(BANDS)], 0) for side in range(2)], 1
            )
            score = dot_nt(one_head(query, second), key) + bias
            weight = jnp.exp(score)
            prob = weight * (1.0 / jnp.sum(weight, -1, keepdims=True))
            prob_b = prob.astype(bf16)
            probs.append(prob)
            probs_b.append(prob_b)
            part = dot(prob_b, one_head(value, second))
            total = part if total is None else total + part
        mixed.append(total.astype(bf16))
    mixed = jnp.concatenate(mixed, 1)

    resid = x + dot(mixed, w_out_ref[...])
    gain_mlp = gain_row(gain_mlp_ref)
    unit_two, inverse_two = norm(resid)
    normed_two = (unit_two * gain_mlp).astype(bf16)
    hidden = dot(normed_two, w_fc1_ref[...])
    active, slope = gelu_and_slope(hidden)
    active = active.astype(bf16)
    w_fc2_copy.wait()
    output = resid + dot(active, w_fc2_ref[...])

    cot = jnp.concatenate([group[128:] for group in groups], 0).astype(bf16)
    d_fc2 = dot_tn(active, cot)
    for block in range(3):
        here = d_fc2[:, block * LANES : (block + 1) * LANES].reshape(PLACES, FF // PLACES, LANES)
        halves_ref[1, :, FC2_AT + block * 96 : FC2_AT + block * 96 + 96, :] = here.astype(bf16)
    d_hidden = (dot_nt(cot, w_fc2_ref[...]) * slope).astype(bf16)
    store_columns(halves_ref, 0, FC1_AT, dot_tn(normed_two, d_hidden))
    d_normed_two = dot_nt(d_hidden, w_fc1_ref[...])
    d_values, d_gain_mlp = norm_back(d_normed_two, gain_mlp, unit_two, inverse_two)
    d_resid = cot.astype(f32) + d_values
    d_resid_b = d_resid.astype(bf16)
    d_out = dot_tn(mixed, d_resid_b)
    d_mixed = dot_nt(d_resid_b, w_out_ref[...]).astype(bf16)

    d_queries, d_keys, d_values_ = [], [], []
    rel_rows = []
    for pair in range(HEADS // 2):
        query, key, value = (pair_of(projected, part, pair) for part in range(3))
        query = query * jnp.bfloat16(SCALE)
        d_mixed_pair = pair_of(d_mixed, 0, pair)
        d_query = d_key = d_value = None
        for second in range(2):
            head = 2 * pair + second
            prob, prob_b = probs[head], probs_b[head]
            d_mixed_here = one_head(d_mixed_pair, second)
            d_prob = dot_nt(d_mixed_here, value)
            d_score = prob * (d_prob - jnp.sum(prob * d_prob, -1, keepdims=True))
            sums = []
            for first in range(6):
                tile = None
                for band in range(BANDS):
                    for side in range(2):
                        if 2 * side - band + 3 == first:
                            here = d_score[band * SECTORS : (band + 1) * SECTORS, side * LANES : (side + 1) * LANES]
                            tile = here if tile is None else tile + here
                for step in range(7):
                    sums.append(jnp.sum(jnp.where(apart == (step - 3) % SECTORS, tile, 0.0), 0, keepdims=True))
            none = jnp.zeros((7, LANES), f32)
            sums = jnp.concatenate(sums, 0)
            taps = jnp.concatenate([jnp.where(low, sums, 0.0), none], 0) + jnp.concatenate(
                [none, jnp.where(low, 0.0, sums)], 0
            )
            rel_rows.append(jnp.concatenate([taps, jnp.zeros((LANES - 49, LANES), f32)], 0))
            d_score_b = d_score.astype(bf16)
            parts = (
                dot(d_score_b, one_head(key, second)),
                dot_tn(d_score_b, one_head(query, second)),
                dot_tn(prob_b, d_mixed_here),
            )
            if d_query is None:
                d_query, d_key, d_value = parts
            else:
                d_query, d_key, d_value = d_query + parts[0], d_key + parts[1], d_value + parts[2]
        d_queries.append((d_query * SCALE).astype(bf16))
        d_keys.append(d_key.astype(bf16))
        d_values_.append(d_value.astype(bf16))
    d_proj = jnp.concatenate(d_queries + d_keys + d_values_, 1)
    d_qkv = dot_tn(normed, d_proj)
    store_columns(halves_ref, 0, QKV_AT, d_qkv[:, : QKV_FIRST * LANES])
    store_columns(halves_ref, 1, OUT_AT, jnp.concatenate([d_out, d_qkv[:, QKV_FIRST * LANES :]], 1))
    d_normed = dot_nt(d_proj, w_qkv_ref[...])
    d_flat, d_gain_attn = norm_back(d_normed, gain_attn, unit, inverse)
    d_latent = d_resid + d_flat

    gains = [g[:, k * LANES : (k + 1) * LANES] for g in (d_gain_attn, d_gain_mlp) for k in range(3)]
    rel = lax.dot_general(
        jnp.ones((8, LANES), f32), jnp.concatenate(rel_rows, 0), (((1,), (1,)), ((), ())),
        precision=lax.Precision.HIGHEST, preferred_element_type=f32,
    )
    rel_rows = [rel[:1, head * LANES : (head + 1) * LANES] for head in range(HEADS)]
    small = jnp.concatenate(rel_rows + [jnp.zeros((2, LANES), f32)] + gains + [jnp.zeros((2, LANES), f32)], 0)
    halves_ref[0, 0, SMALL_AT:GRADS, :] = small.astype(bf16)
    halves_ref[0, 1:, SMALL_AT:GRADS, :] = jnp.zeros((PLACES - 1, GRADS - SMALL_AT, LANES), bf16)
    halves_ref[1, :, SMALL_AT:GRADS, :] = jnp.zeros((PLACES, GRADS - SMALL_AT, LANES), bf16)
    for band in range(BANDS):
        y_lo, core = band // 2, band % 2
        rows = slice(band * SECTORS, (band + 1) * SECTORS)
        for block in range(3):
            lanes = slice(block * LANES, (block + 1) * LANES)
            both = jnp.concatenate([a[rows, lanes].reshape(8, DEPTH, LANES) for a in (output, d_latent)], 1)
            at = GRADS + block * 16
            halves_ref[core, y_lo * 8 : y_lo * 8 + 8, at : at + 16, :] = both.astype(bf16)
    core = core_ref[0]
    kept_ref[...] = halves_ref[core]
    sent_ref[...] = halves_ref[1 - core]


SCALAR = pl.BlockSpec(memory_space=pltpu.SMEM)
WHOLE = pl.BlockSpec(memory_space=pltpu.VMEM)


def call(kernel, outs, operands, interpret, room=16, scalars=0, scratch=(), near=True, loose=0):
    tight = len(operands) - loose
    shapes = tuple((pltpu.VMEM if near and not interpret else jax.ShapeDtypeStruct)(s, t) for s, t, near in outs)
    if not interpret:
        places = [pltpu.VMEM if near else pltpu.HBM] * (tight - scalars) + [pltpu.HBM] * loose
        operands = operands[:scalars] + tuple(map(pltpu.with_memory_space_constraint, operands[scalars:], places))
    return pl.pallas_call(
        kernel,
        out_shape=shapes,
        in_specs=[SCALAR] * scalars + [WHOLE] * (tight - scalars) + [pl.BlockSpec(memory_space=pltpu.HBM)] * loose,
        out_specs=(WHOLE,) * len(outs),
        scratch_shapes=scratch,
        compiler_params=pltpu.CompilerParams(vmem_limit_bytes=room * 1024 * 1024),
        interpret=interpret,
    )(*operands)


def block(core, both, gain_attn, w_qkv, rel_bias, w_out, gain_mlp, w_fc1, w_fc2, interpret=False):
    half = (PLACES, GRADS + OWN, LANES)
    return call(
        block_kernel,
        ((half, bf16, True), (half, bf16, True)),
        (core, both, gain_attn, w_qkv, rel_bias, w_out, gain_mlp, w_fc1, w_fc2),
        interpret,
        room=32,
        scalars=1,
        scratch=[pltpu.VMEM((2, *half), bf16), pltpu.VMEM(w_fc2.shape, bf16), pltpu.SemaphoreType.DMA],
        loose=1,
    )


def merge_kernel(core_ref, kept_ref, arrived_ref, out_ref):
    total = kept_ref[:, :GRADS, :].astype(f32) + arrived_ref[:, :GRADS, :].astype(f32)
    out_ref[:, :GRADS, :] = total.astype(bf16)

    def cells(first, second):
        out_ref[:, GRADS : GRADS + OWN, :] = first[:, GRADS:, :]
        out_ref[:, GRADS + OWN :, :] = second[:, GRADS:, :]

    @pl.when(core_ref[0] == 0)
    def _():
        cells(kept_ref, arrived_ref)

    @pl.when(core_ref[0] != 0)
    def _():
        cells(arrived_ref, kept_ref)


def merge(core, kept, arrived, interpret=False):
    out = ((PLACES, GRADS + 2 * OWN, LANES), bf16, True)
    return call(merge_kernel, (out,), (core, kept, arrived), interpret, scalars=1)[0]


def plane_kernel(arrived_ref, out_ref):
    total = arrived_ref[0, :GRADS, :].astype(f32)
    for place in range(1, PLACES):
        total = total + arrived_ref[place, :GRADS, :].astype(f32)
    room = jnp.zeros((DEPTH, PART_ROOM - PART, LANES), f32)
    out_ref[:, :PART_ROOM, :] = jnp.concatenate([total.reshape(DEPTH, PART, LANES), room], 1).astype(bf16)
    blocks = []
    for block in range(3):
        at = GRADS + block * 16
        blocks.append(
            jnp.concatenate([arrived_ref[:, at + c * OWN : at + c * OWN + 16, :].reshape(256, LANES) for c in range(2)], 0)
        )
    rows = jnp.concatenate(blocks, 1)
    moved = reorder(rows, lambda to: bits(to, 0, 1) << 8 | bits(to, 1, 4) << 4 | bits(to, 5, 1) << 3 | to >> 6)
    moved = moved.astype(bf16).reshape(DEPTH, 2, 32, 3 * LANES)
    for array in range(2):
        for block in range(3):
            at = PART_ROOM + (array * 3 + block) * 32
            out_ref[:, at : at + 32, :] = moved[:, array, :, block * LANES : (block + 1) * LANES]


def plane(arrived, interpret=False):
    return call(plane_kernel, (((DEPTH, PART_ROOM + 192, LANES), bf16, True),), (arrived,), interpret)[0]


def depth_kernel(arrived_ref, part_ref, output_ref, d_latent_ref):
    total = jnp.sum(arrived_ref[:, :PART_ROOM, :].astype(f32), 0)[:PART]
    part_ref[...] = jnp.broadcast_to(total[None], (DEPTH, PART, LANES)).astype(bf16)
    for array, ref in enumerate((output_ref, d_latent_ref)):
        starts = [PART_ROOM + (array * 3 + block) * 32 for block in range(3)]
        rows = jnp.concatenate([arrived_ref[:, at : at + 32, :].reshape(CELLS, LANES) for at in starts], 1)
        moved = reorder(rows, lambda to: bits(to, 0, 3) << 5 | bits(to, 7, 1) << 4 | bits(to, 3, 3) << 1 | bits(to, 6, 1))
        ref[...] = moved.astype(bf16)


def depth(arrived, interpret=False):
    cells = ((CELLS, D), bf16, False)
    return call(depth_kernel, (((DEPTH, PART, LANES), bf16, True), cells, cells), (arrived,), interpret)


def half_columns(half, at, block, rows):
    first = at + block // 2 * rows
    start = block % 2 * 8
    return half[start : start + 8, first : first + rows, :].astype(f32).reshape(8 * rows, LANES)


def lanes(block):
    return slice(block * LANES, (block + 1) * LANES)


def write_half(which, half_ref, outs, rooms, sems):
    d_qkv_ref, d_out_ref, d_fc1_ref, d_fc2_ref = outs
    fc1_room, fc2_room, qkv_room, out_room = rooms
    split = QKV_FIRST * LANES

    @pl.when(which == 0)
    def _():
        copies = []
        for part in range(3):
            for block in range(4 * part, 4 * part + 4):
                fc1_room[:, lanes(block)] = half_columns(half_ref, FC1_AT, block, 48)
            columns = pl.ds(part * 4 * LANES, 4 * LANES)
            copies.append(pltpu.make_async_copy(fc1_room.at[:, columns], d_fc1_ref.at[:, columns], sems.at[part]))
            copies[-1].start()
        for block in range(QKV_FIRST):
            qkv_room[:, lanes(block)] = half_columns(half_ref, QKV_AT, block, 48)
        columns = pl.ds(0, split)
        copies.append(pltpu.make_async_copy(qkv_room.at[:, columns], d_qkv_ref.at[:, columns], sems.at[3]))
        copies[-1].start()
        for copy in copies:
            copy.wait()

    @pl.when(which != 0)
    def _():
        copies = []
        for block in range(3):
            at = FC2_AT + block * 96
            fc2_room[:, lanes(block)] = half_ref[:, at : at + 96, :].astype(f32).reshape(FF, LANES)
            columns = pl.ds(block * LANES, LANES)
            copies.append(pltpu.make_async_copy(fc2_room.at[:, columns], d_fc2_ref.at[:, columns], sems.at[block]))
            copies[-1].start()
        for block in range(QKV_FIRST, 9):
            qkv_room[:, lanes(block)] = half_columns(half_ref, OUT_AT, block - QKV_FIRST + 3, 48)
        columns = pl.ds(split, 3 * D - split)
        copies.append(pltpu.make_async_copy(qkv_room.at[:, columns], d_qkv_ref.at[:, columns], sems.at[3]))
        copies[-1].start()
        for block in range(3):
            out_room[:, lanes(block)] = half_columns(half_ref, OUT_AT, block, 48)
        copies.append(pltpu.make_async_copy(out_room, d_out_ref, sems.at[4]))
        copies[-1].start()
        for copy in copies:
            copy.wait()


def near_kernel(core_ref, here_ref, *refs):
    write_half(core_ref[0], here_ref, refs[:4], refs[4:8], refs[8])


def far_kernel(core_ref, here_ref, other_ref, *refs):
    outs, (d_rel_ref, d_gain_attn_ref, d_gain_mlp_ref), rooms, sems = refs[4:8], refs[8:11], refs[11:15], refs[15]
    first = jnp.where(core_ref[0] == 0, here_ref[0, SMALL_AT:GRADS, :], other_ref[0, SMALL_AT:GRADS, :])
    small = first.astype(f32)
    for step in range(7):
        d_rel_ref[:, step, :] = pltpu.roll(small, (LANES - 7 * step) % LANES, 1)[:HEADS, :7]
    for block in range(3):
        d_gain_attn_ref[lanes(block)] = small[8 + block]
        d_gain_mlp_ref[lanes(block)] = small[11 + block]
    write_half(1 - core_ref[0], other_ref, outs, rooms, sems)


def assemble(core, here, other):
    shapes = ((D, 3 * D), (D, D), (D, FF), (FF, D))
    large = tuple(jax.ShapeDtypeStruct(s, f32) for s in shapes)
    small = tuple(jax.ShapeDtypeStruct(s, f32) for s in ((HEADS, 7, 7), (D,), (D,)))
    rooms = [pltpu.VMEM(s, f32) for s in ((D, FF), (FF, D), (D, 3 * D), (D, D))] + [pltpu.SemaphoreType.DMA((5,))]
    far_away = pl.BlockSpec(memory_space=pl.ANY)
    options = pltpu.CompilerParams(vmem_limit_bytes=16 * 1024 * 1024)
    here = pltpu.with_memory_space_constraint(here, pltpu.VMEM)
    begun = pl.pallas_call(
        near_kernel,
        out_shape=large,
        in_specs=[SCALAR, WHOLE],
        out_specs=(far_away,) * 4,
        scratch_shapes=rooms,
        compiler_params=options,
    )(core, here)
    return pl.pallas_call(
        far_kernel,
        out_shape=large + small,
        in_specs=[SCALAR, WHOLE, WHOLE] + [far_away] * 4,
        out_specs=(far_away,) * 4 + (WHOLE,) * 3,
        scratch_shapes=rooms,
        input_output_aliases={3: 0, 4: 1, 5: 2, 6: 3},
        compiler_params=options,
    )(core, here, pltpu.with_memory_space_constraint(other, pltpu.VMEM), *begun)


def exchange(value, axes):
    return lax.all_to_all(value, axes, 0, 0)


def to_sibling(value):
    return lax.ppermute(value, "core", [(0, 1), (1, 0)])


def per_device(latent, cotangent, gain_attn, w_qkv, rel_bias, w_out, gain_mlp, w_fc1, w_fc2):
    shape = latent.shape
    core = lax.axis_index("core").reshape(1)
    gain_attn, w_qkv, rel_bias, w_out, gain_mlp, w_fc1 = fetch(gain_attn, w_qkv, rel_bias, w_out, gain_mlp, w_fc1)
    arrived = exchange(pack(latent, cotangent), AXES)
    kept, sent = block(core, arrived, gain_attn, w_qkv, rel_bias, w_out, gain_mlp, w_fc1, w_fc2)
    merged = merge(core, kept, to_sibling(sent))
    part, output, d_latent = depth(exchange(plane(exchange(merged, PLANE)), "z"))
    piece = exchange(part, "z").reshape(GRADS, LANES)
    here = exchange(jnp.broadcast_to(piece, (PLACES, GRADS, LANES)), PLANE)
    return (output.reshape(shape), d_latent.reshape(shape)) + assemble(core, here, to_sibling(here))


def solution(mesh):
    split = Mesh(mesh.devices.reshape(2, 2, 2, 4, 8), AXES)
    cells = P(("y_lo", "core"), ("y_hi", "x", "z"), None)
    return jax.shard_map(
        per_device,
        mesh=split,
        in_specs=(cells, cells) + (P(),) * 7,
        out_specs=(cells, cells) + (P(),) * 7,
        check_vma=False,
    )
```

```python
import jax
import jax.numpy as jnp
from jax import lax
from jax.experimental import pallas as pl
from jax.experimental.pallas import tpu as pltpu
from jax.sharding import Mesh, PartitionSpec as P

HEADS = 6
HEAD = 64
D = 384
FF = 1536
BANDS = 4
SECTORS = 64
CELLS = BANDS * SECTORS
SCALE = HEAD ** (-0.5)
ABSENT = -1e30
AXES = ("y_lo", "core", "y_hi", "x", "z")
PLANE = ("y_lo", "y_hi", "x")

LANES = 128
PLACES = 16
DEPTH = 8
GRADS = 448
PART = GRADS // DEPTH
OWN = 48
PART_ROOM = 64
ROOM = PART_ROOM + 96
FC1_AT, QKV_AT = 0, 288
FC2_AT, OUT_AT, QKV_REST_AT = 0, 288, 360
SMALL_AT = 432
QKV_FIRST = 6

f32, bf16 = jnp.float32, jnp.bfloat16


def dot(a, b):
    return lax.dot_general(a, b, (((1,), (0,)), ((), ())), preferred_element_type=f32)


def dot_nt(a, b):
    return lax.dot_general(a, b, (((1,), (1,)), ((), ())), preferred_element_type=f32)


def dot_tn(a, b):
    return lax.dot_general(a, b, (((0,), (0,)), ((), ())), preferred_element_type=f32)


def norm(values):
    centred = values - jnp.mean(values, -1, keepdims=True)
    inverse = lax.rsqrt(jnp.mean(centred * centred, -1, keepdims=True) + 1e-05)
    return centred * inverse, inverse


def norm_back(d_normed, gain, unit, inverse):
    d_unit = d_normed * gain
    d_values = inverse * (
        d_unit
        - jnp.mean(d_unit, -1, keepdims=True)
        - unit * jnp.mean(d_unit * unit, -1, keepdims=True)
    )
    return d_values, jnp.sum(d_normed * unit, 0, keepdims=True)


def gelu_and_slope(x):
    root = 0.7978845608028654
    square = x * x
    t = jnp.tanh(root * x * (1.0 + 0.044715 * square))
    half = 0.5 * (1.0 + t)
    slope = half + (0.5 * root) * x * (1.0 - t * t) * (1.0 + 3.0 * 0.044715 * square)
    return x * half, slope


def store_columns(ref, half, at, values):
    rows = values.shape[0] // 8
    for block in range(values.shape[1] // LANES):
        here = values[:, block * LANES : (block + 1) * LANES].reshape(8, rows, LANES)
        first = at + block // 2 * rows
        start = block % 2 * 8
        ref[half, start : start + 8, first : first + rows, :] = here.astype(bf16)


def bits(number, low, count):
    return (number >> low) & ((1 << count) - 1)


def reorder(rows, source):
    count = rows.shape[0]
    to = lax.broadcasted_iota(jnp.int32, (count, count), 0)
    chosen = jnp.where(lax.broadcasted_iota(jnp.int32, (count, count), 1) == source(to), 1.0, 0.0).astype(bf16)
    return dot(chosen, rows)


def pack_kernel(latent_ref, cot_ref, out_ref):
    for start in range(0, CELLS, 128):
        parts = [ref[start // 16 : start // 16 + 8].reshape(128, D) for ref in (latent_ref, cot_ref)]
        rows = reorder(jnp.concatenate(parts, 0), lambda to: bits(to, 0, 1) << 7 | to >> 1)
        out_ref[start : start + 128] = rows.astype(bf16).reshape(128, 2, D)


def pack(latent, cot, interpret=False):
    return call(pack_kernel, (((CELLS, 2, D), bf16, True),), (latent, cot), interpret, near=False)[0]


def fetch_kernel(*refs):
    count = len(refs) // 2
    sems = refs[-1]
    copies = [pltpu.make_async_copy(refs[i], refs[count + i], sems.at[i]) for i in range(count)]
    for copy in copies:
        copy.start()
    for copy in copies:
        copy.wait()


def fetch(*arrays):
    return pl.pallas_call(
        fetch_kernel,
        out_shape=tuple(pltpu.VMEM(a.shape, a.dtype) for a in arrays),
        in_specs=[pl.BlockSpec(memory_space=pltpu.HBM)] * len(arrays),
        out_specs=(WHOLE,) * len(arrays),
        scratch_shapes=[pltpu.SemaphoreType.DMA((len(arrays),))],
        compiler_params=pltpu.CompilerParams(vmem_limit_bytes=1024 * 1024),
    )(*(pltpu.with_memory_space_constraint(a, pltpu.HBM) for a in arrays))


def gain_row(ref):
    return jnp.concatenate([ref[lanes(block)].reshape(1, LANES) for block in range(3)], 1)


def block_kernel(core_ref, both_ref, gain_attn_ref, w_qkv_ref, bias_ref, w_out_ref, gain_mlp_ref, w_fc1_ref, w_fc2_far_ref,
                 kept_ref, sent_ref, halves_ref, w_fc2_ref, sem):
    w_fc2_copy = pltpu.make_async_copy(w_fc2_far_ref, w_fc2_ref, sem)
    w_fc2_copy.start()
    groups = [both_ref[start : start + 128].reshape(256, D) for start in range(0, CELLS, 128)]
    groups = [reorder(group, lambda to: bits(to, 0, 7) << 1 | to >> 7) for group in groups]
    x = jnp.concatenate([group[:128] for group in groups], 0)
    gain_attn = gain_row(gain_attn_ref)
    unit, inverse = norm(x)
    normed = (unit * gain_attn).astype(bf16)
    projected = dot(normed, w_qkv_ref[...]).astype(bf16)

    lane = lax.broadcasted_iota(jnp.int32, (1, LANES), 1)
    low = lane < HEAD
    apart = (
        lax.broadcasted_iota(jnp.int32, (SECTORS, LANES), 1)
        - lax.broadcasted_iota(jnp.int32, (SECTORS, LANES), 0)
    ) & (SECTORS - 1)

    same = lax.broadcasted_iota(jnp.int32, (7, 7), 0) == lax.broadcasted_iota(jnp.int32, (7, 7), 1)
    bias_rows = []
    for head in range(HEADS):
        table = bias_ref[head]
        columns = [jnp.sum(jnp.where(same, table[band : band + 1], 0.0), 1, keepdims=True) for band in range(7)]
        bias_rows.append([jnp.where(low, columns[first], columns[first + 1]) for first in range(6)])

    def one_head(pair, second):
        return jnp.where(low, jnp.bfloat16(0), pair) if second else jnp.where(low, pair, jnp.bfloat16(0))

    def pair_of(array, part, pair):
        start = part * D + pair * LANES
        return array[:, start : start + LANES]

    probs, probs_b, mixed = [], [], []
    for pair in range(HEADS // 2):
        query, key, value = (pair_of(projected, part, pair) for part in range(3))
        query = query * jnp.bfloat16(SCALE)
        total = None
        for second in range(2):
            head = 2 * pair + second
            tiles = []
            for first in range(6):
                tile = jnp.full((SECTORS, LANES), ABSENT, f32)
                for step in range(7):
                    row = bias_rows[head][first][step : step + 1]
                    tile = jnp.where(apart == (step - 3) % SECTORS, row, tile)
                tiles.append(tile)
            bias = jnp.concatenate(
                [jnp.concatenate([tiles[2 * side - band + 3] for band in range(BANDS)], 0) for side in range(2)], 1
            )
            score = dot_nt(one_head(query, second), key) + bias
            weight = jnp.exp(score)
            prob = weight * (1.0 / jnp.sum(weight, -1, keepdims=True))
            prob_b = prob.astype(bf16)
            probs.append(prob)
            probs_b.append(prob_b)
            part = dot(prob_b, one_head(value, second))
            total = part if total is None else total + part
        mixed.append(total.astype(bf16))
    mixed = jnp.concatenate(mixed, 1)

    resid = x + dot(mixed, w_out_ref[...])
    gain_mlp = gain_row(gain_mlp_ref)
    unit_two, inverse_two = norm(resid)
    normed_two = (unit_two * gain_mlp).astype(bf16)
    hidden = dot(normed_two, w_fc1_ref[...])
    active, slope = gelu_and_slope(hidden)
    active = active.astype(bf16)
    w_fc2_copy.wait()
    output = resid + dot(active, w_fc2_ref[...])

    cot = jnp.concatenate([group[128:] for group in groups], 0).astype(bf16)
    d_fc2 = dot_tn(active, cot)
    for block in range(3):
        here = d_fc2[:, block * LANES : (block + 1) * LANES].reshape(PLACES, FF // PLACES, LANES)
        halves_ref[1, :, FC2_AT + block * 96 : FC2_AT + block * 96 + 96, :] = here.astype(bf16)
    d_hidden = (dot_nt(cot, w_fc2_ref[...]) * slope).astype(bf16)
    store_columns(halves_ref, 0, FC1_AT, dot_tn(normed_two, d_hidden))
    d_normed_two = dot_nt(d_hidden, w_fc1_ref[...])
    d_values, d_gain_mlp = norm_back(d_normed_two, gain_mlp, unit_two, inverse_two)
    d_resid = cot.astype(f32) + d_values
    d_resid_b = d_resid.astype(bf16)
    d_out = dot_tn(mixed, d_resid_b)
    d_mixed = dot_nt(d_resid_b, w_out_ref[...]).astype(bf16)

    d_queries, d_keys, d_values_ = [], [], []
    rel_rows = []
    for pair in range(HEADS // 2):
        query, key, value = (pair_of(projected, part, pair) for part in range(3))
        query = query * jnp.bfloat16(SCALE)
        d_mixed_pair = pair_of(d_mixed, 0, pair)
        d_query = d_key = d_value = None
        for second in range(2):
            head = 2 * pair + second
            prob, prob_b = probs[head], probs_b[head]
            d_mixed_here = one_head(d_mixed_pair, second)
            d_prob = dot_nt(d_mixed_here, value)
            d_score = prob * (d_prob - jnp.sum(prob * d_prob, -1, keepdims=True))
            sums = []
            for first in range(6):
                tile = None
                for band in range(BANDS):
                    for side in range(2):
                        if 2 * side - band + 3 == first:
                            here = d_score[band * SECTORS : (band + 1) * SECTORS, side * LANES : (side + 1) * LANES]
                            tile = here if tile is None else tile + here
                for step in range(7):
                    sums.append(jnp.sum(jnp.where(apart == (step - 3) % SECTORS, tile, 0.0), 0, keepdims=True))
            none = jnp.zeros((7, LANES), f32)
            sums = jnp.concatenate(sums, 0)
            taps = jnp.concatenate([jnp.where(low, sums, 0.0), none], 0) + jnp.concatenate(
                [none, jnp.where(low, 0.0, sums)], 0
            )
            rel_rows.append(jnp.concatenate([taps, jnp.zeros((LANES - 49, LANES), f32)], 0))
            d_score_b = d_score.astype(bf16)
            parts = (
                dot(d_score_b, one_head(key, second)),
                dot_tn(d_score_b, one_head(query, second)),
                dot_tn(prob_b, d_mixed_here),
            )
            if d_query is None:
                d_query, d_key, d_value = parts
            else:
                d_query, d_key, d_value = d_query + parts[0], d_key + parts[1], d_value + parts[2]
        d_queries.append((d_query * SCALE).astype(bf16))
        d_keys.append(d_key.astype(bf16))
        d_values_.append(d_value.astype(bf16))
    d_proj = jnp.concatenate(d_queries + d_keys + d_values_, 1)
    d_qkv = dot_tn(normed, d_proj)
    store_columns(halves_ref, 0, QKV_AT, d_qkv[:, : QKV_FIRST * LANES])
    store_columns(halves_ref, 1, OUT_AT, jnp.concatenate([d_out, d_qkv[:, QKV_FIRST * LANES :]], 1))
    d_normed = dot_nt(d_proj, w_qkv_ref[...])
    d_flat, d_gain_attn = norm_back(d_normed, gain_attn, unit, inverse)
    d_latent = d_resid + d_flat

    gains = [g[:, k * LANES : (k + 1) * LANES] for g in (d_gain_attn, d_gain_mlp) for k in range(3)]
    rel = lax.dot_general(
        jnp.ones((8, LANES), f32), jnp.concatenate(rel_rows, 0), (((1,), (1,)), ((), ())),
        precision=lax.Precision.HIGHEST, preferred_element_type=f32,
    )
    rel_rows = [rel[:1, head * LANES : (head + 1) * LANES] for head in range(HEADS)]
    small = jnp.concatenate(rel_rows + [jnp.zeros((2, LANES), f32)] + gains + [jnp.zeros((2, LANES), f32)], 0)
    halves_ref[0, 0, SMALL_AT:GRADS, :] = small.astype(bf16)
    halves_ref[0, 1:, SMALL_AT:GRADS, :] = jnp.zeros((PLACES - 1, GRADS - SMALL_AT, LANES), bf16)
    halves_ref[1, :, SMALL_AT:GRADS, :] = jnp.zeros((PLACES, GRADS - SMALL_AT, LANES), bf16)
    for band in range(BANDS):
        y_lo, core = band // 2, band % 2
        rows = slice(band * SECTORS, (band + 1) * SECTORS)
        for block in range(3):
            lanes = slice(block * LANES, (block + 1) * LANES)
            both = jnp.concatenate([a[rows, lanes].reshape(8, DEPTH, LANES) for a in (output, d_latent)], 1)
            at = GRADS + block * 16
            halves_ref[core, y_lo * 8 : y_lo * 8 + 8, at : at + 16, :] = both.astype(bf16)
    core = core_ref[0]
    kept_ref[...] = halves_ref[core]
    sent_ref[...] = halves_ref[1 - core]


SCALAR = pl.BlockSpec(memory_space=pltpu.SMEM)
WHOLE = pl.BlockSpec(memory_space=pltpu.VMEM)


def call(kernel, outs, operands, interpret, room=16, scalars=0, scratch=(), near=True, loose=0):
    tight = len(operands) - loose
    shapes = tuple((pltpu.VMEM if near and not interpret else jax.ShapeDtypeStruct)(s, t) for s, t, near in outs)
    if not interpret:
        places = [pltpu.VMEM if near else pltpu.HBM] * (tight - scalars) + [pltpu.HBM] * loose
        operands = operands[:scalars] + tuple(map(pltpu.with_memory_space_constraint, operands[scalars:], places))
    return pl.pallas_call(
        kernel,
        out_shape=shapes,
        in_specs=[SCALAR] * scalars + [WHOLE] * (tight - scalars) + [pl.BlockSpec(memory_space=pltpu.HBM)] * loose,
        out_specs=(WHOLE,) * len(outs),
        scratch_shapes=scratch,
        compiler_params=pltpu.CompilerParams(vmem_limit_bytes=room * 1024 * 1024),
        interpret=interpret,
    )(*operands)


def block(core, both, gain_attn, w_qkv, rel_bias, w_out, gain_mlp, w_fc1, w_fc2, interpret=False):
    half = (PLACES, GRADS + OWN, LANES)
    return call(
        block_kernel,
        ((half, bf16, True), (half, bf16, True)),
        (core, both, gain_attn, w_qkv, rel_bias, w_out, gain_mlp, w_fc1, w_fc2),
        interpret,
        room=32,
        scalars=1,
        scratch=[pltpu.VMEM((2, *half), bf16), pltpu.VMEM(w_fc2.shape, bf16), pltpu.SemaphoreType.DMA],
        loose=1,
    )


def merge_kernel(core_ref, kept_ref, arrived_ref, out_ref):
    total = kept_ref[:, :GRADS, :].astype(f32) + arrived_ref[:, :GRADS, :].astype(f32)
    out_ref[:, :GRADS, :] = total.astype(bf16)

    def cells(first, second):
        out_ref[:, GRADS : GRADS + OWN, :] = first[:, GRADS:, :]
        out_ref[:, GRADS + OWN :, :] = second[:, GRADS:, :]

    @pl.when(core_ref[0] == 0)
    def _():
        cells(kept_ref, arrived_ref)

    @pl.when(core_ref[0] != 0)
    def _():
        cells(arrived_ref, kept_ref)


def merge(core, kept, arrived, interpret=False):
    out = ((PLACES, GRADS + 2 * OWN, LANES), bf16, True)
    return call(merge_kernel, (out,), (core, kept, arrived), interpret, scalars=1)[0]


def plane_kernel(arrived_ref, out_ref, later_ref):
    total = arrived_ref[0, :GRADS, :].astype(f32)
    for place in range(1, PLACES):
        total = total + arrived_ref[place, :GRADS, :].astype(f32)
    room = jnp.zeros((DEPTH, PART_ROOM - PART, LANES), f32)
    out_ref[:, :PART_ROOM, :] = jnp.concatenate([total.reshape(DEPTH, PART, LANES), room], 1).astype(bf16)
    blocks = []
    for block in range(3):
        at = GRADS + block * 16
        blocks.append(
            jnp.concatenate([arrived_ref[:, at + c * OWN : at + c * OWN + 16, :].reshape(256, LANES) for c in range(2)], 0)
        )
    rows = jnp.concatenate(blocks, 1)
    moved = reorder(rows, lambda to: bits(to, 0, 1) << 8 | bits(to, 1, 4) << 4 | bits(to, 5, 1) << 3 | to >> 6)
    moved = moved.astype(bf16).reshape(DEPTH, 2, 32, 3 * LANES)
    for array, (ref, start) in enumerate(((out_ref, PART_ROOM), (later_ref, 0))):
        for block in range(3):
            at = start + block * 32
            ref[:, at : at + 32, :] = moved[:, array, :, block * LANES : (block + 1) * LANES]


def plane(arrived, interpret=False):
    outs = (((DEPTH, ROOM, LANES), bf16, True), ((DEPTH, ROOM - PART_ROOM, LANES), bf16, True))
    return call(plane_kernel, outs, (arrived,), interpret)


def depth_kernel(arrived_ref, later_ref, out_ref):
    total = jnp.sum(arrived_ref[:, :PART_ROOM, :].astype(f32), 0)
    out_ref[:, :PART_ROOM, :] = jnp.broadcast_to(total[None], (DEPTH, PART_ROOM, LANES)).astype(bf16)
    out_ref[:, PART_ROOM:, :] = later_ref[...]


def depth(arrived, later, interpret=False):
    return call(depth_kernel, (((DEPTH, ROOM, LANES), bf16, True),), (arrived, later), interpret)[0]


def spread_kernel(arrived_ref, out_ref):
    parts = arrived_ref[:, :PART_ROOM, :].astype(f32)[:, :PART]
    piece = parts.reshape(GRADS, LANES).astype(bf16)
    for place in range(PLACES):
        out_ref[place] = piece


def spread(arrived, interpret=False):
    return call(spread_kernel, (((PLACES, GRADS, LANES), bf16, True),), (arrived,), interpret)[0]


def half_columns(half, at, block, rows):
    first = at + block // 2 * rows
    start = block % 2 * 8
    return half[start : start + 8, first : first + rows, :].astype(f32).reshape(8 * rows, LANES)


def lanes(block):
    return slice(block * LANES, (block + 1) * LANES)


def write_half(which, half_ref, outs, rooms, sems):
    d_qkv_ref, d_out_ref, d_fc1_ref, d_fc2_ref = outs
    fc1_room, fc2_room, qkv_room, out_room = rooms
    split = QKV_FIRST * LANES

    @pl.when(which == 0)
    def _():
        copies = []
        for part in range(3):
            for block in range(4 * part, 4 * part + 4):
                fc1_room[:, lanes(block)] = half_columns(half_ref, FC1_AT, block, 48)
            columns = pl.ds(part * 4 * LANES, 4 * LANES)
            copies.append(pltpu.make_async_copy(fc1_room.at[:, columns], d_fc1_ref.at[:, columns], sems.at[part]))
            copies[-1].start()
        for block in range(QKV_FIRST):
            qkv_room[:, lanes(block)] = half_columns(half_ref, QKV_AT, block, 48)
        columns = pl.ds(0, split)
        copies.append(pltpu.make_async_copy(qkv_room.at[:, columns], d_qkv_ref.at[:, columns], sems.at[3]))
        copies[-1].start()
        for copy in copies:
            copy.wait()

    @pl.when(which != 0)
    def _():
        copies = []
        for block in range(3):
            at = FC2_AT + block * 96
            fc2_room[:, lanes(block)] = half_ref[:, at : at + 96, :].astype(f32).reshape(FF, LANES)
            columns = pl.ds(block * LANES, LANES)
            copies.append(pltpu.make_async_copy(fc2_room.at[:, columns], d_fc2_ref.at[:, columns], sems.at[block]))
            copies[-1].start()
        for block in range(QKV_FIRST, 9):
            qkv_room[:, lanes(block)] = half_columns(half_ref, OUT_AT, block - QKV_FIRST + 3, 48)
        columns = pl.ds(split, 3 * D - split)
        copies.append(pltpu.make_async_copy(qkv_room.at[:, columns], d_qkv_ref.at[:, columns], sems.at[3]))
        copies[-1].start()
        for block in range(3):
            out_room[:, lanes(block)] = half_columns(half_ref, OUT_AT, block, 48)
        copies.append(pltpu.make_async_copy(out_room, d_out_ref, sems.at[4]))
        copies[-1].start()
        for copy in copies:
            copy.wait()


def near_kernel(core_ref, here_ref, output_ref, d_latent_ref, *refs):
    for cells_ref, ref in zip((output_ref, d_latent_ref), refs[4:6]):
        starts = [PART_ROOM + block * 32 for block in range(3)]
        rows = jnp.concatenate([cells_ref[:, at : at + 32, :].reshape(CELLS, LANES) for at in starts], 1)
        moved = reorder(rows, lambda to: bits(to, 0, 3) << 5 | bits(to, 7, 1) << 4 | bits(to, 3, 3) << 1 | bits(to, 6, 1))
        ref[...] = moved.astype(bf16)
    write_half(core_ref[0], here_ref, refs[:4], refs[6:10], refs[10])


def far_kernel(core_ref, here_ref, other_ref, *refs):
    outs, (d_rel_ref, d_gain_attn_ref, d_gain_mlp_ref), rooms, sems = refs[4:8], refs[8:11], refs[11:15], refs[15]
    first = jnp.where(core_ref[0] == 0, here_ref[0, SMALL_AT:GRADS, :], other_ref[0, SMALL_AT:GRADS, :])
    small = first.astype(f32)
    for step in range(7):
        d_rel_ref[:, step, :] = pltpu.roll(small, (LANES - 7 * step) % LANES, 1)[:HEADS, :7]
    for block in range(3):
        d_gain_attn_ref[lanes(block)] = small[8 + block]
        d_gain_mlp_ref[lanes(block)] = small[11 + block]
    write_half(1 - core_ref[0], other_ref, outs, rooms, sems)


def assemble(core, here, other, *cells):
    shapes = ((D, 3 * D), (D, D), (D, FF), (FF, D))
    large = tuple(jax.ShapeDtypeStruct(s, f32) for s in shapes)
    small = tuple(jax.ShapeDtypeStruct(s, f32) for s in ((HEADS, 7, 7), (D,), (D,)))
    rooms = [pltpu.VMEM(s, f32) for s in ((D, FF), (FF, D), (D, 3 * D), (D, D))] + [pltpu.SemaphoreType.DMA((5,))]
    far_away = pl.BlockSpec(memory_space=pl.ANY)
    options = pltpu.CompilerParams(vmem_limit_bytes=16 * 1024 * 1024)
    here = pltpu.with_memory_space_constraint(here, pltpu.VMEM)
    begun = pl.pallas_call(
        near_kernel,
        out_shape=large + (jax.ShapeDtypeStruct((CELLS, D), bf16),) * 2,
        in_specs=[SCALAR] + [WHOLE] * 3,
        out_specs=(far_away,) * 4 + (WHOLE,) * 2,
        scratch_shapes=rooms,
        compiler_params=options,
    )(core, here, *(pltpu.with_memory_space_constraint(c, pltpu.VMEM) for c in cells))
    return begun[4:], pl.pallas_call(
        far_kernel,
        out_shape=large + small,
        in_specs=[SCALAR, WHOLE, WHOLE] + [far_away] * 4,
        out_specs=(far_away,) * 4 + (WHOLE,) * 3,
        scratch_shapes=rooms,
        input_output_aliases={3: 0, 4: 1, 5: 2, 6: 3},
        compiler_params=options,
    )(core, here, pltpu.with_memory_space_constraint(other, pltpu.VMEM), *begun[:4])


def exchange(value, axes):
    return lax.all_to_all(value, axes, 0, 0)


def to_sibling(value):
    return lax.ppermute(value, "core", [(0, 1), (1, 0)])


def per_device(latent, cotangent, gain_attn, w_qkv, rel_bias, w_out, gain_mlp, w_fc1, w_fc2):
    shape = latent.shape
    core = lax.axis_index("core").reshape(1)
    gain_attn, w_qkv, rel_bias, w_out, gain_mlp, w_fc1 = fetch(gain_attn, w_qkv, rel_bias, w_out, gain_mlp, w_fc1)
    arrived = exchange(pack(latent, cotangent), AXES)
    kept, sent = block(core, arrived, gain_attn, w_qkv, rel_bias, w_out, gain_mlp, w_fc1, w_fc2)
    merged = merge(core, kept, to_sibling(sent))
    parts, later = plane(exchange(merged, PLANE))
    first = exchange(parts, "z")
    second = exchange(depth(first, later), "z")
    here = exchange(spread(second), PLANE)
    (output, d_latent), grads = assemble(core, here, to_sibling(here), first, second)
    return (output.reshape(shape), d_latent.reshape(shape)) + grads


def solution(mesh):
    split = Mesh(mesh.devices.reshape(2, 2, 2, 4, 8), AXES)
    cells = P(("y_lo", "core"), ("y_hi", "x", "z"), None)
    return jax.shard_map(
        per_device,
        mesh=split,
        in_specs=(cells, cells) + (P(),) * 7,
        out_specs=(cells, cells) + (P(),) * 7,
        check_vma=False,
    )
```

```python
import jax
import jax.numpy as jnp
from jax import lax
from jax.experimental import pallas as pl
from jax.experimental.pallas import tpu as pltpu
from jax.sharding import Mesh, PartitionSpec as P

HEADS = 6
HEAD = 64
D = 384
FF = 1536
BANDS = 4
SECTORS = 64
CELLS = BANDS * SECTORS
SCALE = HEAD ** (-0.5)
ABSENT = -1e30
AXES = ("y_lo", "core", "y_hi", "x", "z")
PLANE = ("y_lo", "y_hi", "x")

LANES = 128
PLACES = 16
DEPTH = 8
GRADS = 448
PART = GRADS // DEPTH
OWN = 48
PART_ROOM = 64
ROOM = PART_ROOM + 96
FC1_AT, QKV_AT = 0, 288
FC2_AT, OUT_AT, QKV_REST_AT = 0, 288, 360
SMALL_AT = 432
QKV_FIRST = 6

f32, bf16 = jnp.float32, jnp.bfloat16


def dot(a, b):
    return lax.dot_general(a, b, (((1,), (0,)), ((), ())), preferred_element_type=f32)


def dot_nt(a, b):
    return lax.dot_general(a, b, (((1,), (1,)), ((), ())), preferred_element_type=f32)


def dot_tn(a, b):
    return lax.dot_general(a, b, (((0,), (0,)), ((), ())), preferred_element_type=f32)


def norm(values):
    centred = values - jnp.mean(values, -1, keepdims=True)
    inverse = lax.rsqrt(jnp.mean(centred * centred, -1, keepdims=True) + 1e-05)
    return centred * inverse, inverse


def norm_back(d_normed, gain, unit, inverse):
    d_unit = d_normed * gain
    d_values = inverse * (
        d_unit
        - jnp.mean(d_unit, -1, keepdims=True)
        - unit * jnp.mean(d_unit * unit, -1, keepdims=True)
    )
    return d_values, jnp.sum(d_normed * unit, 0, keepdims=True)


def gelu_and_slope(x):
    root = 0.7978845608028654
    square = x * x
    t = jnp.tanh(root * x * (1.0 + 0.044715 * square))
    half = 0.5 * (1.0 + t)
    slope = half + (0.5 * root) * x * (1.0 - t * t) * (1.0 + 3.0 * 0.044715 * square)
    return x * half, slope


def store_columns(ref, half, at, values):
    rows = values.shape[0] // 8
    for block in range(values.shape[1] // LANES):
        here = values[:, block * LANES : (block + 1) * LANES].reshape(8, rows, LANES)
        first = at + block // 2 * rows
        start = block % 2 * 8
        ref[half, start : start + 8, first : first + rows, :] = here.astype(bf16)


def bits(number, low, count):
    return (number >> low) & ((1 << count) - 1)


def reorder(rows, source):
    count = rows.shape[0]
    to = lax.broadcasted_iota(jnp.int32, (count, count), 0)
    chosen = jnp.where(lax.broadcasted_iota(jnp.int32, (count, count), 1) == source(to), 1.0, 0.0).astype(bf16)
    return dot(chosen, rows)


def pack_kernel(latent_ref, cot_ref, out_ref):
    for start in range(0, CELLS, 128):
        parts = [ref[start // 16 : start // 16 + 8].reshape(128, D) for ref in (latent_ref, cot_ref)]
        rows = reorder(jnp.concatenate(parts, 0), lambda to: bits(to, 0, 1) << 7 | to >> 1)
        out_ref[start : start + 128] = rows.astype(bf16).reshape(128, 2, D)


def pack(latent, cot, interpret=False):
    return call(pack_kernel, (((CELLS, 2, D), bf16, True),), (latent, cot), interpret, near=False)[0]


def fetch_kernel(*refs):
    count = len(refs) // 2
    sems = refs[-1]
    copies = [pltpu.make_async_copy(refs[i], refs[count + i], sems.at[i]) for i in range(count)]
    for copy in copies:
        copy.start()
    for copy in copies:
        copy.wait()


def fetch(*arrays):
    return pl.pallas_call(
        fetch_kernel,
        out_shape=tuple(pltpu.VMEM(a.shape, a.dtype) for a in arrays),
        in_specs=[pl.BlockSpec(memory_space=pltpu.HBM)] * len(arrays),
        out_specs=(WHOLE,) * len(arrays),
        scratch_shapes=[pltpu.SemaphoreType.DMA((len(arrays),))],
        compiler_params=pltpu.CompilerParams(vmem_limit_bytes=1024 * 1024),
    )(*(pltpu.with_memory_space_constraint(a, pltpu.HBM) for a in arrays))


def gain_row(ref):
    return jnp.concatenate([ref[lanes(block)].reshape(1, LANES) for block in range(3)], 1)


def block_kernel(core_ref, both_ref, gain_attn_ref, w_qkv_ref, bias_ref, w_out_ref, gain_mlp_ref, w_fc1_ref, w_fc2_far_ref,
                 kept_ref, sent_ref, halves_ref, w_fc2_ref, sem):
    w_fc2_copy = pltpu.make_async_copy(w_fc2_far_ref, w_fc2_ref, sem)
    w_fc2_copy.start()
    groups = [both_ref[start : start + 128].reshape(256, D) for start in range(0, CELLS, 128)]
    groups = [reorder(group, lambda to: bits(to, 0, 7) << 1 | to >> 7) for group in groups]
    x = jnp.concatenate([group[:128] for group in groups], 0)
    gain_attn = gain_row(gain_attn_ref)
    unit, inverse = norm(x)
    normed = (unit * gain_attn).astype(bf16)
    projected = dot(normed, w_qkv_ref[...]).astype(bf16)

    lane = lax.broadcasted_iota(jnp.int32, (1, LANES), 1)
    low = lane < HEAD
    apart = (
        lax.broadcasted_iota(jnp.int32, (SECTORS, LANES), 1)
        - lax.broadcasted_iota(jnp.int32, (SECTORS, LANES), 0)
    ) & (SECTORS - 1)

    same = lax.broadcasted_iota(jnp.int32, (7, 7), 0) == lax.broadcasted_iota(jnp.int32, (7, 7), 1)
    bias_rows = []
    for head in range(HEADS):
        table = bias_ref[head]
        columns = [jnp.sum(jnp.where(same, table[band : band + 1], 0.0), 1, keepdims=True) for band in range(7)]
        bias_rows.append([jnp.where(low, columns[first], columns[first + 1]) for first in range(6)])

    def one_head(pair, second):
        return jnp.where(low, jnp.bfloat16(0), pair) if second else jnp.where(low, pair, jnp.bfloat16(0))

    def pair_of(array, part, pair):
        start = part * D + pair * LANES
        return array[:, start : start + LANES]

    probs, probs_b, mixed = [], [], []
    for pair in range(HEADS // 2):
        query, key, value = (pair_of(projected, part, pair) for part in range(3))
        query = query * jnp.bfloat16(SCALE)
        total = None
        for second in range(2):
            head = 2 * pair + second
            tiles = []
            for first in range(6):
                tile = jnp.full((SECTORS, LANES), ABSENT, f32)
                for step in range(7):
                    row = bias_rows[head][first][step : step + 1]
                    tile = jnp.where(apart == (step - 3) % SECTORS, row, tile)
                tiles.append(tile)
            bias = jnp.concatenate(
                [jnp.concatenate([tiles[2 * side - band + 3] for band in range(BANDS)], 0) for side in range(2)], 1
            )
            score = dot_nt(one_head(query, second), key) + bias
            weight = jnp.exp(score)
            prob = weight * (1.0 / jnp.sum(weight, -1, keepdims=True))
            prob_b = prob.astype(bf16)
            probs.append(prob)
            probs_b.append(prob_b)
            part = dot(prob_b, one_head(value, second))
            total = part if total is None else total + part
        mixed.append(total.astype(bf16))
    mixed = jnp.concatenate(mixed, 1)

    resid = x + dot(mixed, w_out_ref[...])
    gain_mlp = gain_row(gain_mlp_ref)
    unit_two, inverse_two = norm(resid)
    normed_two = (unit_two * gain_mlp).astype(bf16)
    hidden = dot(normed_two, w_fc1_ref[...])
    active, slope = gelu_and_slope(hidden)
    active = active.astype(bf16)
    w_fc2_copy.wait()
    output = resid + dot(active, w_fc2_ref[...])

    cot = jnp.concatenate([group[128:] for group in groups], 0).astype(bf16)
    d_fc2 = dot_tn(active, cot)
    for block in range(3):
        here = d_fc2[:, block * LANES : (block + 1) * LANES].reshape(PLACES, FF // PLACES, LANES)
        halves_ref[1, :, FC2_AT + block * 96 : FC2_AT + block * 96 + 96, :] = here.astype(bf16)
    d_hidden = (dot_nt(cot, w_fc2_ref[...]) * slope).astype(bf16)
    store_columns(halves_ref, 0, FC1_AT, dot_tn(normed_two, d_hidden))
    d_normed_two = dot_nt(d_hidden, w_fc1_ref[...])
    d_values, d_gain_mlp = norm_back(d_normed_two, gain_mlp, unit_two, inverse_two)
    d_resid = cot.astype(f32) + d_values
    d_resid_b = d_resid.astype(bf16)
    d_out = dot_tn(mixed, d_resid_b)
    d_mixed = dot_nt(d_resid_b, w_out_ref[...]).astype(bf16)

    d_queries, d_keys, d_values_ = [], [], []
    rel_rows = []
    for pair in range(HEADS // 2):
        query, key, value = (pair_of(projected, part, pair) for part in range(3))
        query = query * jnp.bfloat16(SCALE)
        d_mixed_pair = pair_of(d_mixed, 0, pair)
        d_query = d_key = d_value = None
        for second in range(2):
            head = 2 * pair + second
            prob, prob_b = probs[head], probs_b[head]
            d_mixed_here = one_head(d_mixed_pair, second)
            d_prob = dot_nt(d_mixed_here, value)
            d_score = prob * (d_prob - jnp.sum(prob * d_prob, -1, keepdims=True))
            sums = []
            for first in range(6):
                tile = None
                for band in range(BANDS):
                    for side in range(2):
                        if 2 * side - band + 3 == first:
                            here = d_score[band * SECTORS : (band + 1) * SECTORS, side * LANES : (side + 1) * LANES]
                            tile = here if tile is None else tile + here
                for step in range(7):
                    sums.append(jnp.sum(jnp.where(apart == (step - 3) % SECTORS, tile, 0.0), 0, keepdims=True))
            none = jnp.zeros((7, LANES), f32)
            sums = jnp.concatenate(sums, 0)
            taps = jnp.concatenate([jnp.where(low, sums, 0.0), none], 0) + jnp.concatenate(
                [none, jnp.where(low, 0.0, sums)], 0
            )
            rel_rows.append(jnp.concatenate([taps, jnp.zeros((LANES - 49, LANES), f32)], 0))
            d_score_b = d_score.astype(bf16)
            parts = (
                dot(d_score_b, one_head(key, second)),
                dot_tn(d_score_b, one_head(query, second)),
                dot_tn(prob_b, d_mixed_here),
            )
            if d_query is None:
                d_query, d_key, d_value = parts
            else:
                d_query, d_key, d_value = d_query + parts[0], d_key + parts[1], d_value + parts[2]
        d_queries.append((d_query * SCALE).astype(bf16))
        d_keys.append(d_key.astype(bf16))
        d_values_.append(d_value.astype(bf16))
    d_proj = jnp.concatenate(d_queries + d_keys + d_values_, 1)
    d_qkv = dot_tn(normed, d_proj)
    store_columns(halves_ref, 0, QKV_AT, d_qkv[:, : QKV_FIRST * LANES])
    store_columns(halves_ref, 1, OUT_AT, jnp.concatenate([d_out, d_qkv[:, QKV_FIRST * LANES :]], 1))
    d_normed = dot_nt(d_proj, w_qkv_ref[...])
    d_flat, d_gain_attn = norm_back(d_normed, gain_attn, unit, inverse)
    d_latent = d_resid + d_flat

    gains = [g[:, k * LANES : (k + 1) * LANES] for g in (d_gain_attn, d_gain_mlp) for k in range(3)]
    rel = lax.dot_general(
        jnp.ones((8, LANES), f32), jnp.concatenate(rel_rows, 0), (((1,), (1,)), ((), ())),
        precision=lax.Precision.HIGHEST, preferred_element_type=f32,
    )
    rel_rows = [rel[:1, head * LANES : (head + 1) * LANES] for head in range(HEADS)]
    small = jnp.concatenate(rel_rows + [jnp.zeros((2, LANES), f32)] + gains + [jnp.zeros((2, LANES), f32)], 0)
    halves_ref[0, 0, SMALL_AT:GRADS, :] = small.astype(bf16)
    halves_ref[0, 1:, SMALL_AT:GRADS, :] = jnp.zeros((PLACES - 1, GRADS - SMALL_AT, LANES), bf16)
    halves_ref[1, :, SMALL_AT:GRADS, :] = jnp.zeros((PLACES, GRADS - SMALL_AT, LANES), bf16)
    for band in range(BANDS):
        y_lo, core = band // 2, band % 2
        rows = slice(band * SECTORS, (band + 1) * SECTORS)
        for block in range(3):
            lanes = slice(block * LANES, (block + 1) * LANES)
            both = jnp.concatenate([a[rows, lanes].reshape(8, DEPTH, LANES) for a in (output, d_latent)], 1)
            at = GRADS + block * 16
            halves_ref[core, y_lo * 8 : y_lo * 8 + 8, at : at + 16, :] = both.astype(bf16)
    core = core_ref[0]
    kept_ref[...] = halves_ref[core]
    sent_ref[...] = halves_ref[1 - core]


SCALAR = pl.BlockSpec(memory_space=pltpu.SMEM)
WHOLE = pl.BlockSpec(memory_space=pltpu.VMEM)


def call(kernel, outs, operands, interpret, room=16, scalars=0, scratch=(), near=True, loose=0):
    tight = len(operands) - loose
    shapes = tuple((pltpu.VMEM if near and not interpret else jax.ShapeDtypeStruct)(s, t) for s, t, near in outs)
    if not interpret:
        places = [pltpu.VMEM if near else pltpu.HBM] * (tight - scalars) + [pltpu.HBM] * loose
        operands = operands[:scalars] + tuple(map(pltpu.with_memory_space_constraint, operands[scalars:], places))
    return pl.pallas_call(
        kernel,
        out_shape=shapes,
        in_specs=[SCALAR] * scalars + [WHOLE] * (tight - scalars) + [pl.BlockSpec(memory_space=pltpu.HBM)] * loose,
        out_specs=(WHOLE,) * len(outs),
        scratch_shapes=scratch,
        compiler_params=pltpu.CompilerParams(vmem_limit_bytes=room * 1024 * 1024),
        interpret=interpret,
    )(*operands)


def block(core, both, gain_attn, w_qkv, rel_bias, w_out, gain_mlp, w_fc1, w_fc2, interpret=False):
    half = (PLACES, GRADS + OWN, LANES)
    return call(
        block_kernel,
        ((half, bf16, True), (half, bf16, True)),
        (core, both, gain_attn, w_qkv, rel_bias, w_out, gain_mlp, w_fc1, w_fc2),
        interpret,
        room=32,
        scalars=1,
        scratch=[pltpu.VMEM((2, *half), bf16), pltpu.VMEM(w_fc2.shape, bf16), pltpu.SemaphoreType.DMA],
        loose=1,
    )


def merge_kernel(core_ref, kept_ref, arrived_ref, out_ref):
    total = kept_ref[:, :GRADS, :].astype(f32) + arrived_ref[:, :GRADS, :].astype(f32)
    out_ref[:, :GRADS, :] = total.astype(bf16)

    def cells(first, second):
        out_ref[:, GRADS : GRADS + OWN, :] = first[:, GRADS:, :]
        out_ref[:, GRADS + OWN :, :] = second[:, GRADS:, :]

    @pl.when(core_ref[0] == 0)
    def _():
        cells(kept_ref, arrived_ref)

    @pl.when(core_ref[0] != 0)
    def _():
        cells(arrived_ref, kept_ref)


def merge(core, kept, arrived, interpret=False):
    out = ((PLACES, GRADS + 2 * OWN, LANES), bf16, True)
    return call(merge_kernel, (out,), (core, kept, arrived), interpret, scalars=1)[0]


def plane_kernel(arrived_ref, out_ref, later_ref):
    total = arrived_ref[0, :GRADS, :].astype(f32)
    for place in range(1, PLACES):
        total = total + arrived_ref[place, :GRADS, :].astype(f32)
    room = jnp.zeros((DEPTH, PART_ROOM - PART, LANES), f32)
    out_ref[:, :PART_ROOM, :] = jnp.concatenate([total.reshape(DEPTH, PART, LANES), room], 1).astype(bf16)
    blocks = []
    for block in range(3):
        at = GRADS + block * 16
        blocks.append(
            jnp.concatenate([arrived_ref[:, at + c * OWN : at + c * OWN + 16, :].reshape(256, LANES) for c in range(2)], 0)
        )
    rows = jnp.concatenate(blocks, 1)
    moved = reorder(rows, lambda to: bits(to, 0, 1) << 8 | bits(to, 1, 4) << 4 | bits(to, 5, 1) << 3 | to >> 6)
    moved = moved.astype(bf16).reshape(DEPTH, 2, 32, 3 * LANES)
    for array, (ref, start) in enumerate(((out_ref, PART_ROOM), (later_ref, 0))):
        for block in range(3):
            at = start + block * 32
            ref[:, at : at + 32, :] = moved[:, array, :, block * LANES : (block + 1) * LANES]


def plane(arrived, interpret=False):
    outs = (((DEPTH, ROOM, LANES), bf16, True), ((DEPTH, ROOM - PART_ROOM, LANES), bf16, True))
    return call(plane_kernel, outs, (arrived,), interpret)


def depth_kernel(arrived_ref, later_ref, out_ref):
    total = jnp.sum(arrived_ref[:, :PART_ROOM, :].astype(f32), 0)
    out_ref[:, :PART_ROOM, :] = jnp.broadcast_to(total[None], (DEPTH, PART_ROOM, LANES)).astype(bf16)
    out_ref[:, PART_ROOM:, :] = later_ref[...]


def depth(arrived, later, interpret=False):
    return call(depth_kernel, (((DEPTH, ROOM, LANES), bf16, True),), (arrived, later), interpret)[0]


def spread_kernel(arrived_ref, out_ref):
    parts = arrived_ref[:, :PART_ROOM, :].astype(f32)[:, :PART]
    piece = parts.reshape(GRADS, LANES).astype(bf16)
    for place in range(PLACES):
        out_ref[place] = piece


def spread(arrived, interpret=False):
    return call(spread_kernel, (((PLACES, GRADS, LANES), bf16, True),), (arrived,), interpret)[0]


def half_columns(half, at, block, rows):
    first = at + block // 2 * rows
    start = block % 2 * 8
    return half[start : start + 8, first : first + rows, :].astype(f32).reshape(8 * rows, LANES)


def lanes(block):
    return slice(block * LANES, (block + 1) * LANES)


def write_half(which, half_ref, outs, rooms, sems):
    d_qkv_ref, d_out_ref, d_fc1_ref, d_fc2_ref = outs
    fc1_room, fc2_room, qkv_room, out_room = rooms
    split = QKV_FIRST * LANES

    @pl.when(which == 0)
    def _():
        copies = []
        for part in range(3):
            for block in range(4 * part, 4 * part + 4):
                fc1_room[:, lanes(block)] = half_columns(half_ref, FC1_AT, block, 48)
            columns = pl.ds(part * 4 * LANES, 4 * LANES)
            copies.append(pltpu.make_async_copy(fc1_room.at[:, columns], d_fc1_ref.at[:, columns], sems.at[part]))
            copies[-1].start()
        for block in range(QKV_FIRST):
            qkv_room[:, lanes(block)] = half_columns(half_ref, QKV_AT, block, 48)
        columns = pl.ds(0, split)
        copies.append(pltpu.make_async_copy(qkv_room.at[:, columns], d_qkv_ref.at[:, columns], sems.at[3]))
        copies[-1].start()
        for copy in copies:
            copy.wait()

    @pl.when(which != 0)
    def _():
        copies = []
        for block in range(3):
            at = FC2_AT + block * 96
            fc2_room[:, lanes(block)] = half_ref[:, at : at + 96, :].astype(f32).reshape(FF, LANES)
            columns = pl.ds(block * LANES, LANES)
            copies.append(pltpu.make_async_copy(fc2_room.at[:, columns], d_fc2_ref.at[:, columns], sems.at[block]))
            copies[-1].start()
        for block in range(QKV_FIRST, 9):
            qkv_room[:, lanes(block)] = half_columns(half_ref, OUT_AT, block - QKV_FIRST + 3, 48)
        columns = pl.ds(split, 3 * D - split)
        copies.append(pltpu.make_async_copy(qkv_room.at[:, columns], d_qkv_ref.at[:, columns], sems.at[3]))
        copies[-1].start()
        for block in range(3):
            out_room[:, lanes(block)] = half_columns(half_ref, OUT_AT, block, 48)
        copies.append(pltpu.make_async_copy(out_room, d_out_ref, sems.at[4]))
        copies[-1].start()
        for copy in copies:
            copy.wait()


def near_kernel(core_ref, here_ref, output_ref, d_latent_ref, *refs):
    for cells_ref, ref in zip((output_ref, d_latent_ref), refs[4:6]):
        starts = [PART_ROOM + block * 32 for block in range(3)]
        rows = jnp.concatenate([cells_ref[:, at : at + 32, :].reshape(CELLS, LANES) for at in starts], 1)
        moved = reorder(rows, lambda to: bits(to, 0, 3) << 5 | bits(to, 7, 1) << 4 | bits(to, 3, 3) << 1 | bits(to, 6, 1))
        ref[...] = moved.astype(bf16)
    write_half(core_ref[0], here_ref, refs[:4], refs[6:10], refs[10])


def far_kernel(core_ref, here_ref, other_ref, *refs):
    outs, small_outs, rooms, sems = refs[4:8], refs[8:11], refs[11:15], refs[15]
    small_rooms, small_sems = refs[16:19], refs[19]
    d_rel_room, d_gain_attn_room, d_gain_mlp_room = small_rooms
    first = jnp.where(core_ref[0] == 0, here_ref[0, SMALL_AT:GRADS, :], other_ref[0, SMALL_AT:GRADS, :])
    small = first.astype(f32)
    for step in range(7):
        d_rel_room[:, step, :] = pltpu.roll(small, (LANES - 7 * step) % LANES, 1)[:HEADS, :7]
    for block in range(3):
        d_gain_attn_room[lanes(block)] = small[8 + block]
        d_gain_mlp_room[lanes(block)] = small[11 + block]
    copies = [pltpu.make_async_copy(small_rooms[i], small_outs[i], small_sems.at[i]) for i in range(3)]
    for copy in copies:
        copy.start()
    write_half(1 - core_ref[0], other_ref, outs, rooms, sems)
    for copy in copies:
        copy.wait()


def assemble(core, here, other, *cells):
    shapes = ((D, 3 * D), (D, D), (D, FF), (FF, D))
    large = tuple(jax.ShapeDtypeStruct(s, f32) for s in shapes)
    small = tuple(jax.ShapeDtypeStruct(s, f32) for s in ((HEADS, 7, 7), (D,), (D,)))
    rooms = [pltpu.VMEM(s, f32) for s in ((D, FF), (FF, D), (D, 3 * D), (D, D))] + [pltpu.SemaphoreType.DMA((5,))]
    far_away = pl.BlockSpec(memory_space=pl.ANY)
    options = pltpu.CompilerParams(vmem_limit_bytes=16 * 1024 * 1024)
    here = pltpu.with_memory_space_constraint(here, pltpu.VMEM)
    begun = pl.pallas_call(
        near_kernel,
        out_shape=large + (jax.ShapeDtypeStruct((CELLS, D), bf16),) * 2,
        in_specs=[SCALAR] + [WHOLE] * 3,
        out_specs=(far_away,) * 4 + (WHOLE,) * 2,
        scratch_shapes=rooms,
        compiler_params=options,
    )(core, here, *(pltpu.with_memory_space_constraint(c, pltpu.VMEM) for c in cells))
    return begun[4:], pl.pallas_call(
        far_kernel,
        out_shape=large + small,
        in_specs=[SCALAR, WHOLE, WHOLE] + [far_away] * 4,
        out_specs=(far_away,) * 7,
        scratch_shapes=rooms
        + [pltpu.VMEM(o.shape, f32) for o in small]
        + [pltpu.SemaphoreType.DMA((3,))],
        input_output_aliases={3: 0, 4: 1, 5: 2, 6: 3},
        compiler_params=options,
    )(core, here, pltpu.with_memory_space_constraint(other, pltpu.VMEM), *begun[:4])


def exchange(value, axes):
    return lax.all_to_all(value, axes, 0, 0)


def to_sibling(value):
    return lax.ppermute(value, "core", [(0, 1), (1, 0)])


def per_device(latent, cotangent, gain_attn, w_qkv, rel_bias, w_out, gain_mlp, w_fc1, w_fc2):
    shape = latent.shape
    core = lax.axis_index("core").reshape(1)
    gain_attn, w_qkv, rel_bias, w_out, gain_mlp, w_fc1 = fetch(gain_attn, w_qkv, rel_bias, w_out, gain_mlp, w_fc1)
    arrived = exchange(pack(latent, cotangent), AXES)
    kept, sent = block(core, arrived, gain_attn, w_qkv, rel_bias, w_out, gain_mlp, w_fc1, w_fc2)
    merged = merge(core, kept, to_sibling(sent))
    parts, later = plane(exchange(merged, PLANE))
    first = exchange(parts, "z")
    second = exchange(depth(first, later), "z")
    here = exchange(spread(second), PLANE)
    (output, d_latent), grads = assemble(core, here, to_sibling(here), first, second)
    return (output.reshape(shape), d_latent.reshape(shape)) + grads


def solution(mesh):
    split = Mesh(mesh.devices.reshape(2, 2, 2, 4, 8), AXES)
    cells = P(("y_lo", "core"), ("y_hi", "x", "z"), None)
    return jax.shard_map(
        per_device,
        mesh=split,
        in_specs=(cells, cells) + (P(),) * 7,
        out_specs=(cells, cells) + (P(),) * 7,
        check_vma=False,
    )
```

```python
import jax
import jax.numpy as jnp
from jax import lax
from jax.experimental import pallas as pl
from jax.experimental.pallas import tpu as pltpu
from jax.sharding import Mesh, PartitionSpec as P

HEADS = 6
HEAD = 64
D = 384
FF = 1536
BANDS = 4
SECTORS = 64
CELLS = BANDS * SECTORS
SCALE = HEAD ** (-0.5)
ABSENT = -1e30
AXES = ("y_lo", "core", "y_hi", "x", "z")
PLANE = ("y_lo", "y_hi", "x")

LANES = 128
PLACES = 16
DEPTH = 8
GRADS = 448
PART = GRADS // DEPTH
OWN = 48
PART_ROOM = 64
ROOM = PART_ROOM + 96
FC1_AT, QKV_AT = 0, 288
FC2_AT, OUT_AT, QKV_REST_AT = 0, 288, 360
SMALL_AT = 432
QKV_FIRST = 6

f32, bf16 = jnp.float32, jnp.bfloat16


def dot(a, b):
    return lax.dot_general(a, b, (((1,), (0,)), ((), ())), preferred_element_type=f32)


def dot_nt(a, b):
    return lax.dot_general(a, b, (((1,), (1,)), ((), ())), preferred_element_type=f32)


def dot_tn(a, b):
    return lax.dot_general(a, b, (((0,), (0,)), ((), ())), preferred_element_type=f32)


def norm(values):
    centred = values - jnp.mean(values, -1, keepdims=True)
    inverse = lax.rsqrt(jnp.mean(centred * centred, -1, keepdims=True) + 1e-05)
    return centred * inverse, inverse


def norm_back(d_normed, gain, unit, inverse):
    d_unit = d_normed * gain
    d_values = inverse * (
        d_unit
        - jnp.mean(d_unit, -1, keepdims=True)
        - unit * jnp.mean(d_unit * unit, -1, keepdims=True)
    )
    return d_values, jnp.sum(d_normed * unit, 0, keepdims=True)


def gelu_and_slope(x):
    root = 0.7978845608028654
    square = x * x
    t = jnp.tanh(root * x * (1.0 + 0.044715 * square))
    half = 0.5 * (1.0 + t)
    slope = half + (0.5 * root) * x * (1.0 - t * t) * (1.0 + 3.0 * 0.044715 * square)
    return x * half, slope


def store_columns(ref, half, at, values):
    rows = values.shape[0] // 8
    for block in range(values.shape[1] // LANES):
        here = values[:, block * LANES : (block + 1) * LANES].reshape(8, rows, LANES)
        first = at + block // 2 * rows
        start = block % 2 * 8
        ref[half, start : start + 8, first : first + rows, :] = here.astype(bf16)


def bits(number, low, count):
    return (number >> low) & ((1 << count) - 1)


def reorder(rows, source):
    count = rows.shape[0]
    to = lax.broadcasted_iota(jnp.int32, (count, count), 0)
    chosen = jnp.where(lax.broadcasted_iota(jnp.int32, (count, count), 1) == source(to), 1.0, 0.0).astype(bf16)
    return dot(chosen, rows)


def pack_kernel(latent_ref, cot_ref, out_ref):
    for start in range(0, CELLS, 128):
        parts = [ref[start // 16 : start // 16 + 8].reshape(128, D) for ref in (latent_ref, cot_ref)]
        rows = reorder(jnp.concatenate(parts, 0), lambda to: bits(to, 0, 1) << 7 | to >> 1)
        out_ref[start : start + 128] = rows.astype(bf16).reshape(128, 2, D)


def pack(latent, cot, interpret=False):
    return call(pack_kernel, (((CELLS, 2, D), bf16, True),), (latent, cot), interpret, near=False)[0]


def fetch_kernel(*refs):
    count = len(refs) // 2
    sems = refs[-1]
    copies = [pltpu.make_async_copy(refs[i], refs[count + i], sems.at[i]) for i in range(count)]
    for copy in copies:
        copy.start()
    for copy in copies:
        copy.wait()


def fetch(*arrays):
    return pl.pallas_call(
        fetch_kernel,
        out_shape=tuple(pltpu.VMEM(a.shape, a.dtype) for a in arrays),
        in_specs=[pl.BlockSpec(memory_space=pltpu.HBM)] * len(arrays),
        out_specs=(WHOLE,) * len(arrays),
        scratch_shapes=[pltpu.SemaphoreType.DMA((len(arrays),))],
        compiler_params=pltpu.CompilerParams(vmem_limit_bytes=1024 * 1024),
    )(*(pltpu.with_memory_space_constraint(a, pltpu.HBM) for a in arrays))


def gain_row(ref):
    return jnp.concatenate([ref[lanes(block)].reshape(1, LANES) for block in range(3)], 1)


def block_kernel(core_ref, both_ref, gain_attn_ref, w_qkv_ref, bias_ref, w_out_ref, gain_mlp_ref, w_fc1_ref, w_fc2_far_ref,
                 kept_ref, sent_ref, halves_ref, w_fc2_ref, sem, move_sems):
    w_fc2_copy = pltpu.make_async_copy(w_fc2_far_ref, w_fc2_ref, sem)
    w_fc2_copy.start()
    groups = [both_ref[start : start + 128].reshape(256, D) for start in range(0, CELLS, 128)]
    groups = [reorder(group, lambda to: bits(to, 0, 7) << 1 | to >> 7) for group in groups]
    x = jnp.concatenate([group[:128] for group in groups], 0)
    gain_attn = gain_row(gain_attn_ref)
    unit, inverse = norm(x)
    normed = (unit * gain_attn).astype(bf16)
    projected = dot(normed, w_qkv_ref[...]).astype(bf16)

    lane = lax.broadcasted_iota(jnp.int32, (1, LANES), 1)
    low = lane < HEAD
    apart = (
        lax.broadcasted_iota(jnp.int32, (SECTORS, LANES), 1)
        - lax.broadcasted_iota(jnp.int32, (SECTORS, LANES), 0)
    ) & (SECTORS - 1)

    same = lax.broadcasted_iota(jnp.int32, (7, 7), 0) == lax.broadcasted_iota(jnp.int32, (7, 7), 1)
    bias_rows = []
    for head in range(HEADS):
        table = bias_ref[head]
        columns = [jnp.sum(jnp.where(same, table[band : band + 1], 0.0), 1, keepdims=True) for band in range(7)]
        bias_rows.append([jnp.where(low, columns[first], columns[first + 1]) for first in range(6)])

    def one_head(pair, second):
        return jnp.where(low, jnp.bfloat16(0), pair) if second else jnp.where(low, pair, jnp.bfloat16(0))

    def pair_of(array, part, pair):
        start = part * D + pair * LANES
        return array[:, start : start + LANES]

    probs, probs_b, mixed = [], [], []
    for pair in range(HEADS // 2):
        query, key, value = (pair_of(projected, part, pair) for part in range(3))
        query = query * jnp.bfloat16(SCALE)
        total = None
        for second in range(2):
            head = 2 * pair + second
            tiles = []
            for first in range(6):
                tile = jnp.full((SECTORS, LANES), ABSENT, f32)
                for step in range(7):
                    row = bias_rows[head][first][step : step + 1]
                    tile = jnp.where(apart == (step - 3) % SECTORS, row, tile)
                tiles.append(tile)
            bias = jnp.concatenate(
                [jnp.concatenate([tiles[2 * side - band + 3] for band in range(BANDS)], 0) for side in range(2)], 1
            )
            score = dot_nt(one_head(query, second), key) + bias
            weight = jnp.exp(score)
            prob = weight * (1.0 / jnp.sum(weight, -1, keepdims=True))
            prob_b = prob.astype(bf16)
            probs.append(prob)
            probs_b.append(prob_b)
            part = dot(prob_b, one_head(value, second))
            total = part if total is None else total + part
        mixed.append(total.astype(bf16))
    mixed = jnp.concatenate(mixed, 1)

    resid = x + dot(mixed, w_out_ref[...])
    gain_mlp = gain_row(gain_mlp_ref)
    unit_two, inverse_two = norm(resid)
    normed_two = (unit_two * gain_mlp).astype(bf16)
    hidden = dot(normed_two, w_fc1_ref[...])
    active, slope = gelu_and_slope(hidden)
    active = active.astype(bf16)
    w_fc2_copy.wait()
    output = resid + dot(active, w_fc2_ref[...])

    cot = jnp.concatenate([group[128:] for group in groups], 0).astype(bf16)
    d_fc2 = dot_tn(active, cot)
    for block in range(3):
        here = d_fc2[:, block * LANES : (block + 1) * LANES].reshape(PLACES, FF // PLACES, LANES)
        halves_ref[1, :, FC2_AT + block * 96 : FC2_AT + block * 96 + 96, :] = here.astype(bf16)
    d_hidden = (dot_nt(cot, w_fc2_ref[...]) * slope).astype(bf16)
    store_columns(halves_ref, 0, FC1_AT, dot_tn(normed_two, d_hidden))
    d_normed_two = dot_nt(d_hidden, w_fc1_ref[...])
    d_values, d_gain_mlp = norm_back(d_normed_two, gain_mlp, unit_two, inverse_two)
    d_resid = cot.astype(f32) + d_values
    d_resid_b = d_resid.astype(bf16)
    d_out = dot_tn(mixed, d_resid_b)
    d_mixed = dot_nt(d_resid_b, w_out_ref[...]).astype(bf16)

    core = core_ref[0]
    done = pl.ds(0, QKV_AT)
    moves = [
        pltpu.make_async_copy(halves_ref.at[core, :, done, :], kept_ref.at[:, done, :], move_sems.at[0]),
        pltpu.make_async_copy(halves_ref.at[1 - core, :, done, :], sent_ref.at[:, done, :], move_sems.at[1]),
    ]
    for move in moves:
        move.start()

    d_queries, d_keys, d_values_ = [], [], []
    rel_rows = []
    for pair in range(HEADS // 2):
        query, key, value = (pair_of(projected, part, pair) for part in range(3))
        query = query * jnp.bfloat16(SCALE)
        d_mixed_pair = pair_of(d_mixed, 0, pair)
        d_query = d_key = d_value = None
        for second in range(2):
            head = 2 * pair + second
            prob, prob_b = probs[head], probs_b[head]
            d_mixed_here = one_head(d_mixed_pair, second)
            d_prob = dot_nt(d_mixed_here, value)
            d_score = prob * (d_prob - jnp.sum(prob * d_prob, -1, keepdims=True))
            sums = []
            for first in range(6):
                tile = None
                for band in range(BANDS):
                    for side in range(2):
                        if 2 * side - band + 3 == first:
                            here = d_score[band * SECTORS : (band + 1) * SECTORS, side * LANES : (side + 1) * LANES]
                            tile = here if tile is None else tile + here
                for step in range(7):
                    sums.append(jnp.sum(jnp.where(apart == (step - 3) % SECTORS, tile, 0.0), 0, keepdims=True))
            none = jnp.zeros((7, LANES), f32)
            sums = jnp.concatenate(sums, 0)
            taps = jnp.concatenate([jnp.where(low, sums, 0.0), none], 0) + jnp.concatenate(
                [none, jnp.where(low, 0.0, sums)], 0
            )
            rel_rows.append(jnp.concatenate([taps, jnp.zeros((LANES - 49, LANES), f32)], 0))
            d_score_b = d_score.astype(bf16)
            parts = (
                dot(d_score_b, one_head(key, second)),
                dot_tn(d_score_b, one_head(query, second)),
                dot_tn(prob_b, d_mixed_here),
            )
            if d_query is None:
                d_query, d_key, d_value = parts
            else:
                d_query, d_key, d_value = d_query + parts[0], d_key + parts[1], d_value + parts[2]
        d_queries.append((d_query * SCALE).astype(bf16))
        d_keys.append(d_key.astype(bf16))
        d_values_.append(d_value.astype(bf16))
    d_proj = jnp.concatenate(d_queries + d_keys + d_values_, 1)
    d_qkv = dot_tn(normed, d_proj)
    store_columns(halves_ref, 0, QKV_AT, d_qkv[:, : QKV_FIRST * LANES])
    store_columns(halves_ref, 1, OUT_AT, jnp.concatenate([d_out, d_qkv[:, QKV_FIRST * LANES :]], 1))
    d_normed = dot_nt(d_proj, w_qkv_ref[...])
    d_flat, d_gain_attn = norm_back(d_normed, gain_attn, unit, inverse)
    d_latent = d_resid + d_flat

    gains = [g[:, k * LANES : (k + 1) * LANES] for g in (d_gain_attn, d_gain_mlp) for k in range(3)]
    rel = lax.dot_general(
        jnp.ones((8, LANES), f32), jnp.concatenate(rel_rows, 0), (((1,), (1,)), ((), ())),
        precision=lax.Precision.HIGHEST, preferred_element_type=f32,
    )
    rel_rows = [rel[:1, head * LANES : (head + 1) * LANES] for head in range(HEADS)]
    small = jnp.concatenate(rel_rows + [jnp.zeros((2, LANES), f32)] + gains + [jnp.zeros((2, LANES), f32)], 0)
    halves_ref[0, 0, SMALL_AT:GRADS, :] = small.astype(bf16)
    halves_ref[0, 1:, SMALL_AT:GRADS, :] = jnp.zeros((PLACES - 1, GRADS - SMALL_AT, LANES), bf16)
    halves_ref[1, :, SMALL_AT:GRADS, :] = jnp.zeros((PLACES, GRADS - SMALL_AT, LANES), bf16)
    for band in range(BANDS):
        y_lo, home = band // 2, band % 2
        rows = slice(band * SECTORS, (band + 1) * SECTORS)
        for block in range(3):
            lanes = slice(block * LANES, (block + 1) * LANES)
            both = jnp.concatenate([a[rows, lanes].reshape(8, DEPTH, LANES) for a in (output, d_latent)], 1)
            at = GRADS + block * 16
            halves_ref[home, y_lo * 8 : y_lo * 8 + 8, at : at + 16, :] = both.astype(bf16)
    core = core_ref[0]
    kept_ref[:, QKV_AT:, :] = halves_ref[core, :, QKV_AT:, :]
    sent_ref[:, QKV_AT:, :] = halves_ref[1 - core, :, QKV_AT:, :]
    for move in moves:
        move.wait()


SCALAR = pl.BlockSpec(memory_space=pltpu.SMEM)
WHOLE = pl.BlockSpec(memory_space=pltpu.VMEM)


def call(kernel, outs, operands, interpret, room=16, scalars=0, scratch=(), near=True, loose=0):
    tight = len(operands) - loose
    shapes = tuple((pltpu.VMEM if near and not interpret else jax.ShapeDtypeStruct)(s, t) for s, t, near in outs)
    if not interpret:
        places = [pltpu.VMEM if near else pltpu.HBM] * (tight - scalars) + [pltpu.HBM] * loose
        operands = operands[:scalars] + tuple(map(pltpu.with_memory_space_constraint, operands[scalars:], places))
    return pl.pallas_call(
        kernel,
        out_shape=shapes,
        in_specs=[SCALAR] * scalars + [WHOLE] * (tight - scalars) + [pl.BlockSpec(memory_space=pltpu.HBM)] * loose,
        out_specs=(WHOLE,) * len(outs),
        scratch_shapes=scratch,
        compiler_params=pltpu.CompilerParams(vmem_limit_bytes=room * 1024 * 1024),
        interpret=interpret,
    )(*operands)


def block(core, both, gain_attn, w_qkv, rel_bias, w_out, gain_mlp, w_fc1, w_fc2, interpret=False):
    half = (PLACES, GRADS + OWN, LANES)
    return call(
        block_kernel,
        ((half, bf16, True), (half, bf16, True)),
        (core, both, gain_attn, w_qkv, rel_bias, w_out, gain_mlp, w_fc1, w_fc2),
        interpret,
        room=32,
        scalars=1,
        scratch=[pltpu.VMEM((2, *half), bf16), pltpu.VMEM(w_fc2.shape, bf16), pltpu.SemaphoreType.DMA]
        + [pltpu.SemaphoreType.DMA((2,))],
        loose=1,
    )


def merge_kernel(core_ref, kept_ref, arrived_ref, out_ref):
    total = kept_ref[:, :GRADS, :].astype(f32) + arrived_ref[:, :GRADS, :].astype(f32)
    out_ref[:, :GRADS, :] = total.astype(bf16)

    def cells(first, second):
        out_ref[:, GRADS : GRADS + OWN, :] = first[:, GRADS:, :]
        out_ref[:, GRADS + OWN :, :] = second[:, GRADS:, :]

    @pl.when(core_ref[0] == 0)
    def _():
        cells(kept_ref, arrived_ref)

    @pl.when(core_ref[0] != 0)
    def _():
        cells(arrived_ref, kept_ref)


def merge(core, kept, arrived, interpret=False):
    out = ((PLACES, GRADS + 2 * OWN, LANES), bf16, True)
    return call(merge_kernel, (out,), (core, kept, arrived), interpret, scalars=1)[0]


def plane_kernel(arrived_ref, out_ref, later_ref):
    total = arrived_ref[0, :GRADS, :].astype(f32)
    for place in range(1, PLACES):
        total = total + arrived_ref[place, :GRADS, :].astype(f32)
    room = jnp.zeros((DEPTH, PART_ROOM - PART, LANES), f32)
    out_ref[:, :PART_ROOM, :] = jnp.concatenate([total.reshape(DEPTH, PART, LANES), room], 1).astype(bf16)
    blocks = []
    for block in range(3):
        at = GRADS + block * 16
        blocks.append(
            jnp.concatenate([arrived_ref[:, at + c * OWN : at + c * OWN + 16, :].reshape(256, LANES) for c in range(2)], 0)
        )
    rows = jnp.concatenate(blocks, 1)
    moved = reorder(rows, lambda to: bits(to, 0, 1) << 8 | bits(to, 1, 4) << 4 | bits(to, 5, 1) << 3 | to >> 6)
    moved = moved.astype(bf16).reshape(DEPTH, 2, 32, 3 * LANES)
    for array, (ref, start) in enumerate(((out_ref, PART_ROOM), (later_ref, 0))):
        for block in range(3):
            at = start + block * 32
            ref[:, at : at + 32, :] = moved[:, array, :, block * LANES : (block + 1) * LANES]


def plane(arrived, interpret=False):
    outs = (((DEPTH, ROOM, LANES), bf16, True), ((DEPTH, ROOM - PART_ROOM, LANES), bf16, True))
    return call(plane_kernel, outs, (arrived,), interpret)


def depth_kernel(arrived_ref, later_ref, out_ref):
    total = jnp.sum(arrived_ref[:, :PART_ROOM, :].astype(f32), 0)
    out_ref[:, :PART_ROOM, :] = jnp.broadcast_to(total[None], (DEPTH, PART_ROOM, LANES)).astype(bf16)
    out_ref[:, PART_ROOM:, :] = later_ref[...]


def depth(arrived, later, interpret=False):
    return call(depth_kernel, (((DEPTH, ROOM, LANES), bf16, True),), (arrived, later), interpret)[0]


def spread_kernel(arrived_ref, out_ref):
    parts = arrived_ref[:, :PART_ROOM, :].astype(f32)[:, :PART]
    piece = parts.reshape(GRADS, LANES).astype(bf16)
    for place in range(PLACES):
        out_ref[place] = piece


def spread(arrived, interpret=False):
    return call(spread_kernel, (((PLACES, GRADS, LANES), bf16, True),), (arrived,), interpret)[0]


def half_columns(half, at, block, rows):
    first = at + block // 2 * rows
    start = block % 2 * 8
    return half[start : start + 8, first : first + rows, :].astype(f32).reshape(8 * rows, LANES)


def lanes(block):
    return slice(block * LANES, (block + 1) * LANES)


def write_half(which, half_ref, outs, rooms, sems):
    d_qkv_ref, d_out_ref, d_fc1_ref, d_fc2_ref = outs
    fc1_room, fc2_room, qkv_room, out_room = rooms
    split = QKV_FIRST * LANES

    @pl.when(which == 0)
    def _():
        copies = []
        for part in range(3):
            for block in range(4 * part, 4 * part + 4):
                fc1_room[:, lanes(block)] = half_columns(half_ref, FC1_AT, block, 48)
            columns = pl.ds(part * 4 * LANES, 4 * LANES)
            copies.append(pltpu.make_async_copy(fc1_room.at[:, columns], d_fc1_ref.at[:, columns], sems.at[part]))
            copies[-1].start()
        for block in range(QKV_FIRST):
            qkv_room[:, lanes(block)] = half_columns(half_ref, QKV_AT, block, 48)
        columns = pl.ds(0, split)
        copies.append(pltpu.make_async_copy(qkv_room.at[:, columns], d_qkv_ref.at[:, columns], sems.at[3]))
        copies[-1].start()
        for copy in copies:
            copy.wait()

    @pl.when(which != 0)
    def _():
        copies = []
        for block in range(3):
            at = FC2_AT + block * 96
            fc2_room[:, lanes(block)] = half_ref[:, at : at + 96, :].astype(f32).reshape(FF, LANES)
            columns = pl.ds(block * LANES, LANES)
            copies.append(pltpu.make_async_copy(fc2_room.at[:, columns], d_fc2_ref.at[:, columns], sems.at[block]))
            copies[-1].start()
        for block in range(QKV_FIRST, 9):
            qkv_room[:, lanes(block)] = half_columns(half_ref, OUT_AT, block - QKV_FIRST + 3, 48)
        columns = pl.ds(split, 3 * D - split)
        copies.append(pltpu.make_async_copy(qkv_room.at[:, columns], d_qkv_ref.at[:, columns], sems.at[3]))
        copies[-1].start()
        for block in range(3):
            out_room[:, lanes(block)] = half_columns(half_ref, OUT_AT, block, 48)
        copies.append(pltpu.make_async_copy(out_room, d_out_ref, sems.at[4]))
        copies[-1].start()
        for copy in copies:
            copy.wait()


def near_kernel(core_ref, here_ref, output_ref, d_latent_ref, *refs):
    for cells_ref, ref in zip((output_ref, d_latent_ref), refs[4:6]):
        starts = [PART_ROOM + block * 32 for block in range(3)]
        rows = jnp.concatenate([cells_ref[:, at : at + 32, :].reshape(CELLS, LANES) for at in starts], 1)
        moved = reorder(rows, lambda to: bits(to, 0, 3) << 5 | bits(to, 7, 1) << 4 | bits(to, 3, 3) << 1 | bits(to, 6, 1))
        ref[...] = moved.astype(bf16)
    write_half(core_ref[0], here_ref, refs[:4], refs[6:10], refs[10])


def far_kernel(core_ref, here_ref, other_ref, *refs):
    outs, small_outs, rooms, sems = refs[4:8], refs[8:11], refs[11:15], refs[15]
    small_rooms, small_sems = refs[16:19], refs[19]
    d_rel_room, d_gain_attn_room, d_gain_mlp_room = small_rooms
    first = jnp.where(core_ref[0] == 0, here_ref[0, SMALL_AT:GRADS, :], other_ref[0, SMALL_AT:GRADS, :])
    small = first.astype(f32)
    for step in range(7):
        d_rel_room[:, step, :] = pltpu.roll(small, (LANES - 7 * step) % LANES, 1)[:HEADS, :7]
    for block in range(3):
        d_gain_attn_room[lanes(block)] = small[8 + block]
        d_gain_mlp_room[lanes(block)] = small[11 + block]
    copies = [pltpu.make_async_copy(small_rooms[i], small_outs[i], small_sems.at[i]) for i in range(3)]
    for copy in copies:
        copy.start()
    write_half(1 - core_ref[0], other_ref, outs, rooms, sems)
    for copy in copies:
        copy.wait()


def assemble(core, here, other, *cells):
    shapes = ((D, 3 * D), (D, D), (D, FF), (FF, D))
    large = tuple(jax.ShapeDtypeStruct(s, f32) for s in shapes)
    small = tuple(jax.ShapeDtypeStruct(s, f32) for s in ((HEADS, 7, 7), (D,), (D,)))
    rooms = [pltpu.VMEM(s, f32) for s in ((D, FF), (FF, D), (D, 3 * D), (D, D))] + [pltpu.SemaphoreType.DMA((5,))]
    far_away = pl.BlockSpec(memory_space=pl.ANY)
    options = pltpu.CompilerParams(vmem_limit_bytes=16 * 1024 * 1024)
    here = pltpu.with_memory_space_constraint(here, pltpu.VMEM)
    begun = pl.pallas_call(
        near_kernel,
        out_shape=large + (jax.ShapeDtypeStruct((CELLS, D), bf16),) * 2,
        in_specs=[SCALAR] + [WHOLE] * 3,
        out_specs=(far_away,) * 4 + (WHOLE,) * 2,
        scratch_shapes=rooms,
        compiler_params=options,
    )(core, here, *(pltpu.with_memory_space_constraint(c, pltpu.VMEM) for c in cells))
    return begun[4:], pl.pallas_call(
        far_kernel,
        out_shape=large + small,
        in_specs=[SCALAR, WHOLE, WHOLE] + [far_away] * 4,
        out_specs=(far_away,) * 7,
        scratch_shapes=rooms
        + [pltpu.VMEM(o.shape, f32) for o in small]
        + [pltpu.SemaphoreType.DMA((3,))],
        input_output_aliases={3: 0, 4: 1, 5: 2, 6: 3},
        compiler_params=options,
    )(core, here, pltpu.with_memory_space_constraint(other, pltpu.VMEM), *begun[:4])


def exchange(value, axes):
    return lax.all_to_all(value, axes, 0, 0)


def to_sibling(value):
    return lax.ppermute(value, "core", [(0, 1), (1, 0)])


def per_device(latent, cotangent, gain_attn, w_qkv, rel_bias, w_out, gain_mlp, w_fc1, w_fc2):
    shape = latent.shape
    core = lax.axis_index("core").reshape(1)
    gain_attn, w_qkv, rel_bias, w_out, gain_mlp, w_fc1 = fetch(gain_attn, w_qkv, rel_bias, w_out, gain_mlp, w_fc1)
    arrived = exchange(pack(latent, cotangent), AXES)
    kept, sent = block(core, arrived, gain_attn, w_qkv, rel_bias, w_out, gain_mlp, w_fc1, w_fc2)
    merged = merge(core, kept, to_sibling(sent))
    parts, later = plane(exchange(merged, PLANE))
    first = exchange(parts, "z")
    second = exchange(depth(first, later), "z")
    here = exchange(spread(second), PLANE)
    (output, d_latent), grads = assemble(core, here, to_sibling(here), first, second)
    return (output.reshape(shape), d_latent.reshape(shape)) + grads


def solution(mesh):
    split = Mesh(mesh.devices.reshape(2, 2, 2, 4, 8), AXES)
    cells = P(("y_lo", "core"), ("y_hi", "x", "z"), None)
    return jax.shard_map(
        per_device,
        mesh=split,
        in_specs=(cells, cells) + (P(),) * 7,
        out_specs=(cells, cells) + (P(),) * 7,
        check_vma=False,
    )
```
